32 devices in a mesh: grp: 2 (over y), pb: 4 (over z), re: 2 (over x), ka: 2 (over core).
Axes of the slice: x: 2, y: 2, z: 4, core: 2. Of those that a mesh axis runs over, the one named last changes fastest.
Arguments:
- g_wann: bfloat16 [2, 1024, 128, 256], P(None, 'pb', ('grp', 're'), 'ka'), parts along dimension 2, may hold values from -0.0234375 to 0.0234375
- phonon_phase: bfloat16 [2, 2048, 1024], P(None, 'pb'), may hold values from -1 to 1, as said below
- electron_phase: bfloat16 [2, 8, 64], replicated, may hold values from -1 to 1, as said below
Outputs:
- coupling: float32 [16, 2, 2048, 256], P(('grp', 're'), None, 'pb', 'ka'), parts along dimension 0
The draws below stay inside these ranges and needn't reach their ends.
There are 2 independent parts, one for each index of `grp`. The reference program is written for one: setup_inputs(seed, part) draws one part's arguments, and reference() takes and returns one part's arrays. A program takes and returns all parts, laid end to end along the dimension named above; an argument that names none is the same for every part. Nothing has to cross between parts.
Inputs may be any that keep to these rules, and one draw needn't show every extreme that they name: `phonon_phase`: entries 0 and 1 along the first dimension are the cosine and sine of one angle. `electron_phase`: entries 0 and 1 along the first dimension are the cosine and sine of one angle.
All inputs are finite; a program needn't handle non-finite values.
Results may differ from the reference program's by a relative error of at most 0.0029.
Values may be sent and summed in bfloat16 or wider, within the bound.
No kernel may reach another device: no remote copies, remote signals or barrier semaphores. Data moves between devices by JAX's collectives and lax.ppermute only.
A program may use at most 64 MiB of HBM per device.

```python
import math
import jax
import jax.numpy as jnp
from jax import lax

BP = 256
RP = 1024
RE = 64
Q = 2048
K = 8


def phase_table(key, rows, vectors):
    key_moment, key_vector = jax.random.split(key)
    moment = jax.random.uniform(key_moment, (rows, 3), jnp.float32)
    picked = jax.random.permutation(key_vector, 4096)[:vectors]
    first = (picked // 256 - 8).astype(jnp.float32)
    second = (picked // 16 % 16 - 8).astype(jnp.float32)
    third = (picked % 16 - 8).astype(jnp.float32)
    product = moment[:, 0:1] * first[None, :] + moment[:, 1:2] * second[None, :] + moment[:, 2:3] * third[None, :]
    angle = 2.0 * math.pi * product
    return jnp.stack([jnp.cos(angle), jnp.sin(angle)]).astype(jnp.bfloat16)


def draw_phonon_phase(key, part):
    return phase_table(jax.random.fold_in(key, 101), Q, RP)


def draw_electron_phase(key, part):
    return phase_table(jax.random.fold_in(key, 202), K, RE)


def levels(key, extent, shards, low, largest):
    loudness = 1.0
    for axis_at, blocks in shards:
        steps = jax.random.uniform(jax.random.fold_in(jax.random.fold_in(key, 6), axis_at), (blocks,), jnp.float32, low / len(shards), largest / len(shards))
        loudness = loudness * jnp.repeat(jnp.exp(steps), extent[axis_at] // blocks).reshape((-1,) + (1,) * (len(extent) - 1 - axis_at))
    return loudness


def centred(stream_key, dims, width, bound, cuts=(), kind=jnp.bfloat16):
    drawn = jax.random.normal(stream_key, dims, jnp.float32) * width
    if len(cuts) > 0:
        drawn = levels(stream_key, dims, cuts, -0.22, 0.18) * drawn
    return jnp.clip(drawn, min=-bound, max=bound).astype(kind)


def setup_inputs(seed: int = 0, part: int = 0) -> dict:
    streams_of = jax.random.split(jax.random.key(seed), 4)
    part_keys = jax.random.split(jax.random.fold_in(streams_of[3], part), 4)
    return {
        "g_wann": centred(part_keys[0], (2, RP, RE, BP), (RE * RP) ** -0.5, 0.0234375, ((1, 4), (2, 2), (3, 2))),
        "phonon_phase": draw_phonon_phase(jax.random.fold_in(streams_of[3], 71), part),
        "electron_phase": draw_electron_phase(jax.random.fold_in(streams_of[3], 71), part),
    }


def reference(g_wann, phonon_phase, electron_phase):
    elec_cos = electron_phase[0].astype(jnp.float32)
    elec_sin = electron_phase[1].astype(jnp.float32)
    wann_real = g_wann[0].astype(jnp.float32)
    wann_imag = g_wann[1].astype(jnp.float32)
    high = lax.Precision.HIGHEST
    bloch_real = jnp.einsum("ke,peb->kpb", elec_cos, wann_real, precision=high) - jnp.einsum("ke,peb->kpb", elec_sin, wann_imag, precision=high)
    bloch_imag = jnp.einsum("ke,peb->kpb", elec_cos, wann_imag, precision=high) + jnp.einsum("ke,peb->kpb", elec_sin, wann_real, precision=high)
    bloch_real = bloch_real.astype(jnp.bfloat16)
    bloch_imag = bloch_imag.astype(jnp.bfloat16)
    cos_table = phonon_phase[0]
    sin_table = phonon_phase[1]

    def one_moment(pair):
        part_real, part_imag = pair
        out_real = jnp.dot(cos_table, part_real, preferred_element_type=jnp.float32) - jnp.dot(sin_table, part_imag, preferred_element_type=jnp.float32)
        out_imag = jnp.dot(cos_table, part_imag, preferred_element_type=jnp.float32) + jnp.dot(sin_table, part_real, preferred_element_type=jnp.float32)
        return jnp.stack([out_real, out_imag])

    return lax.map(one_moment, (bloch_real, bloch_imag))
```

```python
import functools

import jax
import jax.numpy as jnp
from jax import lax
from jax.experimental import pallas as pl
from jax.experimental.pallas import tpu as pltpu
from jax.sharding import PartitionSpec as P

GROUP = 8
CHUNKS = 2


def phase_matrix(phase, n_re):
    k_all, e_all = phase.shape[1:]
    me = lax.axis_index("re")
    e_own, k_own = e_all // n_re, k_all // n_re
    own = lax.dynamic_slice_in_dim(phase, me * e_own, e_own, 2)
    cos, sin = own[0], own[1]
    rows = jnp.stack([jnp.stack([cos, -sin], 1), jnp.stack([sin, cos], 1)])
    rows = rows.reshape(2, n_re, k_own, 2, e_own).transpose(1, 0, 2, 3, 4)
    rows = jnp.roll(rows, -me, 0)
    eye = jnp.eye(GROUP, dtype=phase.dtype)
    big = rows[:, :, :, None, :, None, :] * eye[None, None, None, :, None, :, None]
    return big.reshape(n_re * 2 * k_own * GROUP, 2 * GROUP * e_own)


def electron_kernel(sizes, w_ref, g_ref, *out_refs):
    n_re, k_own = sizes
    p_block, e_own, b = g_ref.shape[1:]
    depth = GROUP * e_own
    for i in range(p_block // GROUP):
        at = pl.ds(i * GROUP, GROUP)
        real = g_ref[0, at].reshape(depth, b)
        imag = g_ref[1, at].reshape(depth, b)
        out = jnp.dot(w_ref[:, :depth], real, preferred_element_type=jnp.float32)
        out += jnp.dot(w_ref[:, depth:], imag, preferred_element_type=jnp.float32)
        out = out.reshape(n_re, 2, k_own, GROUP, b)
        for s in range(n_re):
            first = 0
            for ref in out_refs[s * CHUNKS : (s + 1) * CHUNKS]:
                ref[:, :, at] = out[s, :, first : first + ref.shape[1]]
                first += ref.shape[1]


def electron_sums(weights, g_wann, n_re, k_own, cuts):
    _, p_own, e_own, b = g_wann.shape
    block = min(64, p_own)
    shapes = [jax.ShapeDtypeStruct((2, size, p_own, b), jnp.float32) for _ in range(n_re) for size in cuts]
    outs = pl.pallas_call(
        functools.partial(electron_kernel, (n_re, k_own)),
        grid=(p_own // block,),
        in_specs=[
            pl.BlockSpec(weights.shape, lambda i: (0, 0)),
            pl.BlockSpec((2, block, e_own, b), lambda i: (0, i, 0, 0)),
        ],
        out_specs=[pl.BlockSpec((2, s.shape[1], block, b), lambda i: (0, 0, i, 0)) for s in shapes],
        out_shape=shapes,
        compiler_params=pltpu.CompilerParams(vmem_limit_bytes=32 * 2**20),
        cost_estimate=pl.CostEstimate(flops=2 * 2 * weights.shape[0] * e_own * p_own * b, bytes_accessed=2 * g_wann.size * 2, transcendentals=0),
    )(weights, g_wann)
    return [outs[s * len(cuts) : (s + 1) * len(cuts)] for s in range(n_re)]


def phonon_kernel(n_blocks, sorted_table, order_ref, table_ref, *refs):
    blocks = refs[:n_blocks]
    out_ref = refs[-1]
    p_own, b = blocks[0].shape[2:]
    total = None
    for n, ref in enumerate(blocks):
        at = pl.ds(n * p_own, p_own) if sorted_table else pl.ds(pl.multiple_of(order_ref[n] * p_own, p_own), p_own)
        real, imag = ref[0, 0], ref[1, 0]
        part = jnp.dot(table_ref[0, :, at], jnp.concatenate([real, imag], 1), preferred_element_type=jnp.float32)
        part += jnp.dot(table_ref[1, :, at], jnp.concatenate([-imag, real], 1), preferred_element_type=jnp.float32)
        total = part if total is None else total + part
    out_ref[0, 0] = total[:, :b]
    out_ref[0, 1] = total[:, b:]


def phonon_sums(order, table, blocks, prior, first, k_own):
    _, q, p_all = table.shape
    _, size, p_own, b = blocks[0].shape
    extra = [] if prior is None else [prior]
    sorted_table = p_own % 128 != 0
    if sorted_table:
        table = table.reshape(2, q, len(blocks), p_own)[:, :, order].reshape(table.shape)
    return pl.pallas_call(
        functools.partial(phonon_kernel, len(blocks), sorted_table),
        grid_spec=pltpu.PrefetchScalarGridSpec(
            num_scalar_prefetch=1,
            grid=(size,),
            in_specs=[pl.BlockSpec(table.shape, lambda k, o: (0, 0, 0))]
            + [pl.BlockSpec((2, 1, p_own, b), lambda k, o: (0, k, 0, 0)) for _ in blocks]
            + [pl.BlockSpec(memory_space=pl.ANY) for _ in extra],
            out_specs=pl.BlockSpec((1, 2, q, b), lambda k, o: (first + k, 0, 0, 0)),
        ),
        out_shape=jax.ShapeDtypeStruct((k_own, 2, q, b), jnp.float32),
        input_output_aliases={2 + len(blocks): 0} if extra else {},
        compiler_params=pltpu.CompilerParams(vmem_limit_bytes=32 * 2**20),
        cost_estimate=pl.CostEstimate(flops=8 * q * p_all * b * size, bytes_accessed=table.size * 2 + size * q * b * 8, transcendentals=0),
    )(order, table, *blocks, *extra)


def gather_line(block, n):
    me = lax.axis_index("pb")
    if n == 4:
        near = lax.ppermute(block, "pb", [(i, i ^ 1) for i in range(n)])
        far = lax.ppermute(block, "pb", [(i, i ^ 3) for i in range(n)])
        middle = (me == 1) | (me == 2)
        last = lax.ppermute(jnp.where(middle, far, block), "pb", [(0, 2), (3, 1), (1, 0), (2, 3)])
        order = jnp.stack([me, me ^ 1, me ^ 3, me ^ 2])
        return [block, near, far, last], order
    blocks = [block] + [lax.ppermute(block, "pb", [(i, (i + s) % n) for i in range(n)]) for s in range(1, n)]
    return blocks, jnp.stack([(me - s) % n for s in range(n)])


def body(n_re, n_pb, g_wann, phonon_phase, electron_phase):
    k_own = electron_phase.shape[1] // n_re
    cuts = [k_own // CHUNKS] * CHUNKS
    weights = phase_matrix(electron_phase, n_re)
    partial_sums = electron_sums(weights, g_wann, n_re, k_own, cuts)
    result, first = None, 0
    for c, size in enumerate(cuts):
        total = partial_sums[0][c]
        for s in range(1, n_re):
            total = total + lax.ppermute(partial_sums[s][c], "re", [(i, (i + s) % n_re) for i in range(n_re)])
        blocks, order = gather_line(total.astype(jnp.bfloat16), n_pb)
        result = phonon_sums(order.astype(jnp.int32), phonon_phase, blocks, result, first, k_own)
        first += size
    return result


def solution(mesh):
    return jax.shard_map(
        functools.partial(body, mesh.shape["re"], mesh.shape["pb"]),
        mesh=mesh,
        in_specs=(P(None, "pb", ("grp", "re"), "ka"), P(None, "pb", None), P()),
        out_specs=P(("grp", "re"), None, "pb", "ka"),
        check_vma=False,
    )
```

```python
import functools

import jax
import jax.numpy as jnp
from jax import lax
from jax.experimental import pallas as pl
from jax.experimental.pallas import tpu as pltpu
from jax.sharding import PartitionSpec as P

GROUP = 8
SIDE = 2
PIECES = 4
TAIL = 16
FULL = 32768.0
POWERS = (64, 32, 16, 8, 4, 2)
HEAD = 4
CUTS = (2, 2)
ADDCOST = [0, 10**10, 10**10]
GATES = {('block', 2): [('near', 0), ('far', 0)], ('last', 0): [('near', 0)], ('received', 1): [('block', 0)], ('received', 2): [('block', 0)]}
RELCOST = [0, 0, 0]
PHON = 80
SMALL = 16 * 2**20
LARGE = 50 * 2**20
VMEM = pl.BlockSpec(memory_space=pltpu.VMEM)
HBM = pl.BlockSpec(memory_space=pltpu.HBM)


def pick(me, n, choices):
    out = choices[0]
    for i in range(1, n):
        out = jnp.where(me == i, choices[i], out)
    return out


def phase_rows(me, n_re, phase_ref):
    k_all, e_all = phase_ref.shape[1:]
    e_own, k_own = e_all // n_re, k_all // n_re
    width = GROUP * e_own
    tables = []
    for part in range(2):
        full = phase_ref[part].astype(jnp.float32)
        own = pick(me, n_re, [full[:, r * e_own : (r + 1) * e_own] for r in range(n_re)])
        tables.append(jnp.concatenate([own] * GROUP, 1))
    row = lax.broadcasted_iota(jnp.int32, (k_own * GROUP, width), 0) % GROUP
    column = lax.broadcasted_iota(jnp.int32, (k_own * GROUP, width), 1) // e_own
    spread = []
    for table in tables:
        groups = [table[r * k_own : (r + 1) * k_own] for r in range(n_re)]
        moved = [pick(me, n_re, groups[s:] + groups[:s]) for s in range(n_re)]
        spread.append([
            jnp.where(row == column, jnp.broadcast_to(m[:, None], (k_own, GROUP, width)).reshape(k_own * GROUP, width), 0.0)
            for m in moved
        ])
    cos, sin = spread
    left = jnp.concatenate([x for s in range(n_re) for x in (cos[s], sin[s])], 0)
    right = jnp.concatenate([x for s in range(n_re) for x in (-sin[s], cos[s])], 0)
    return left.astype(jnp.bfloat16), right.astype(jnp.bfloat16)


def electron_kernel(n_re, cuts, pieces, start, phase_ref, g_ref, *refs):
    n = len(cuts)
    own_refs, send_refs = refs[:n], refs[n : n_re * n]
    g_vmem, left_ref, right_ref, sems = refs[n_re * n :]
    _, rows, e_own, b = g_vmem.shape
    size = rows // pieces
    copies = [
        pltpu.make_async_copy(g_ref.at[:, pl.ds(start + i * size, size)], g_vmem.at[:, pl.ds(i * size, size)], sems.at[i])
        for i in range(pieces)
    ]
    for copy in copies:
        copy.start()
    left_ref[...], right_ref[...] = phase_rows(lax.axis_index("re"), n_re, phase_ref)
    depth = GROUP * e_own
    step = SIDE * GROUP
    largest = jnp.zeros((GROUP, b), jnp.float32)
    for i in range(rows // step):
        if i * step % size == 0:
            copies[i * step // size].wait()
        groups = [pl.ds(i * step + j * GROUP, GROUP) for j in range(SIDE)]
        real = jnp.concatenate([g_vmem[0, at].reshape(depth, b) for at in groups], 1)
        imag = jnp.concatenate([g_vmem[1, at].reshape(depth, b) for at in groups], 1)
        out = jnp.dot(left_ref[...], real, preferred_element_type=jnp.float32)
        out += jnp.dot(right_ref[...], imag, preferred_element_type=jnp.float32)
        out = out.reshape(n_re, 2, -1, GROUP, SIDE * b)
        if n_re > 1:
            sent = jnp.max(jnp.abs(out[1:].reshape(-1, GROUP, SIDE * b)), 0)
            for j in range(SIDE):
                largest = jnp.maximum(largest, sent[:, j * b : (j + 1) * b])
        for j, at in enumerate(groups):
            first = 0
            for c, kept in enumerate(cuts):
                own_refs[c][:, :, at] = out[0, :, first : first + kept, :, j * b : (j + 1) * b]
                for s in range(1, n_re):
                    for part in range(2):
                        for k in range(kept):
                            row = (part * kept + k) * rows + i * step + j * GROUP
                            send_refs[(s - 1) * n + c][pl.ds(row, GROUP)] = out[s, part, first + k, :, j * b : (j + 1) * b]
                first += kept
    if n_re > 1:
        top = jnp.max(largest, keepdims=True)
        scale, exponent = jnp.ones((1, 1), jnp.float32), jnp.zeros((1, 1), jnp.float32)
        for bit in POWERS:
            fits = top * scale * 2.0**bit <= FULL
            scale = jnp.where(fits, scale * 2.0**bit, scale)
            exponent = jnp.where(fits, exponent + bit, exponent)
        for ref in send_refs:
            last = ref.shape[0] - TAIL
            ref[pl.ds(0, last)] = ref[pl.ds(0, last)] * scale
            ref[pl.ds(last, TAIL)] = jnp.broadcast_to(exponent, (TAIL, b))


def electron_sums(phase, g_wann, n_re, cuts, start, rows):
    _, _, e_own, b = g_wann.shape
    k_all = phase.shape[1]
    pieces = PIECES if rows % (PIECES * SIDE * GROUP) == 0 else 1
    own = [jax.ShapeDtypeStruct((2, size, rows, b), jnp.float32) for size in cuts]
    send = [jax.ShapeDtypeStruct((2 * size * rows + TAIL, b), jnp.float32) for _ in range(n_re - 1) for size in cuts]
    outs = pl.pallas_call(
        functools.partial(electron_kernel, n_re, cuts, pieces, start),
        in_specs=[VMEM, HBM],
        out_specs=[VMEM] * len(own + send),
        out_shape=own + send,
        scratch_shapes=[
            pltpu.VMEM((2, rows, e_own, b), g_wann.dtype),
            pltpu.VMEM((2 * k_all * GROUP, GROUP * e_own), jnp.bfloat16),
            pltpu.VMEM((2 * k_all * GROUP, GROUP * e_own), jnp.bfloat16),
            pltpu.SemaphoreType.DMA((pieces,)),
        ],
        compiler_params=pltpu.CompilerParams(vmem_limit_bytes=LARGE),
        cost_estimate=pl.CostEstimate(flops=8 * k_all * e_own * rows * b, bytes_accessed=4 * rows * e_own * b, transcendentals=0),
    )(phase, g_wann)
    return outs[: len(cuts)], [outs[s * len(cuts) : (s + 1) * len(cuts)] for s in range(1, n_re)]


def add_kernel(own_ref, *refs):
    out_ref = refs[-1]
    _, kept, rows, _ = own_ref.shape
    factors = []
    for ref in refs[:-1]:
        exponent = ref[pl.ds(ref.shape[0] - TAIL, 1)]
        factor = jnp.ones_like(exponent)
        for bit in POWERS:
            taken = exponent >= bit
            exponent = jnp.where(taken, exponent - bit, exponent)
            factor = jnp.where(taken, factor * 2.0**-bit, factor)
        factors.append(factor)
    for part in range(2):
        for k in range(kept):
            total = own_ref[part, k]
            for ref, factor in zip(refs[:-1], factors):
                total = total + ref[pl.ds((part * kept + k) * rows, rows)] * factor
            out_ref[part, k] = total.astype(out_ref.dtype)


def add_up(own, received, cost):
    return pl.pallas_call(
        add_kernel,
        in_specs=[VMEM] * (1 + len(received)),
        out_specs=VMEM,
        out_shape=jax.ShapeDtypeStruct(own.shape, jnp.bfloat16),
        compiler_params=pltpu.CompilerParams(vmem_limit_bytes=SMALL),
        cost_estimate=pl.CostEstimate(flops=cost, bytes_accessed=0, transcendentals=0),
    )(own, *received)


def block_order(n):
    me = lax.axis_index("pb")
    if n == 4:
        return [me, me ^ 1, me ^ 3, me ^ 2]
    return [(me - s) % n for s in range(n)]


def relay_kernel(block_ref, far_ref, out_ref):
    me = lax.axis_index("pb")
    middle = (me == 1) | (me == 2)
    for c in range(2):
        out_ref[c] = jnp.where(middle, far_ref[c], block_ref[c])


def relay(block, far, cost):
    return pl.pallas_call(
        relay_kernel,
        in_specs=[VMEM, VMEM],
        out_specs=VMEM,
        out_shape=jax.ShapeDtypeStruct(block.shape, block.dtype),
        compiler_params=pltpu.CompilerParams(vmem_limit_bytes=SMALL),
        cost_estimate=pl.CostEstimate(flops=cost, bytes_accessed=0, transcendentals=0),
    )(block, far)


def after(x, *others):
    return lax.optimization_barrier((x, *others))[0] if others else x


def phonon_part(order, table_ref, blocks, first, k):
    total = None
    for n, (head_ref, rest_ref) in enumerate(blocks):
        p_own = head_ref.shape[2] + rest_ref.shape[2]
        at = pl.ds(n * p_own, p_own) if order is None else pl.ds(pl.multiple_of(order[n] * p_own, p_own), p_own)
        real, imag = [jnp.concatenate([head_ref[c, first + k], rest_ref[c, k]], 0) for c in range(2)]
        part = jnp.dot(table_ref[0, :, at], jnp.concatenate([real, imag], 1), preferred_element_type=jnp.float32)
        part += jnp.dot(table_ref[1, :, at], jnp.concatenate([-imag, real], 1), preferred_element_type=jnp.float32)
        total = part if total is None else total + part
    return total


def main_kernel(n, order_of, first, table_ref, *refs):
    blocks = [refs[2 * i : 2 * i + 2] for i in range(n)]
    order, out_ref = order_of(), refs[2 * n]
    for k in range(out_ref.shape[0]):
        out_ref[k] = phonon_part(order, table_ref, blocks, first, k)


def final_kernel(n, order_of, first, has_acc, has_prior, table_ref, *refs):
    blocks = [refs[2 * i : 2 * i + 2] for i in range(n)]
    order = order_of()
    acc_ref = refs[2 * n] if has_acc else None
    out_ref, staged, sems = refs[2 * n + has_acc + has_prior :]
    size, b = staged.shape[0], staged.shape[3]
    copies = []
    for k in range(size):
        total = phonon_part(order, table_ref, blocks, first, k)
        if has_acc:
            total += acc_ref[k]
        staged[k, 0] = total[:, :b]
        staged[k, 1] = total[:, b:]
        copies.append(pltpu.make_async_copy(staged.at[k], out_ref.at[first + k], sems.at[k]))
        copies[-1].start()
    for copy in copies:
        copy.wait()


def phonon_main(order_of, table, blocks, first):
    q = table.shape[1]
    _, size, rows, b = blocks[0][1].shape
    flat = [x for block in blocks for x in block]
    return pl.pallas_call(
        functools.partial(main_kernel, len(blocks), order_of, first),
        in_specs=[VMEM] * (1 + len(flat)),
        out_specs=VMEM,
        out_shape=jax.ShapeDtypeStruct((size, q, 2 * b), jnp.float32),
        compiler_params=pltpu.CompilerParams(vmem_limit_bytes=SMALL),
        cost_estimate=pl.CostEstimate(flops=PHON * q * rows * len(blocks) * b * size, bytes_accessed=0, transcendentals=0),
    )(table, *flat)


def phonon_final(order_of, table, blocks, acc, prior, first, k_own):
    q = table.shape[1]
    _, size, rows, b = blocks[0][1].shape
    flat = [x for block in blocks for x in block]
    more = [] if acc is None else [acc]
    alias = [] if prior is None else [prior]
    return pl.pallas_call(
        functools.partial(final_kernel, len(blocks), order_of, first, len(more), len(alias)),
        in_specs=[VMEM] * (1 + len(flat) + len(more)) + [HBM] * len(alias),
        out_specs=HBM,
        out_shape=jax.ShapeDtypeStruct((k_own, 2, q, b), jnp.float32),
        scratch_shapes=[pltpu.VMEM((size, 2, q, b), jnp.float32), pltpu.SemaphoreType.DMA((size,))],
        input_output_aliases={1 + len(flat) + len(more): 0} if alias else {},
        compiler_params=pltpu.CompilerParams(vmem_limit_bytes=SMALL),
        cost_estimate=pl.CostEstimate(flops=PHON * q * rows * len(blocks) * b * size, bytes_accessed=size * q * b * 8, transcendentals=0),
    )(table, *flat, *more, *alias)


class Transfers:
    def __init__(self, n_re, n_pb, own, send):
        self.n_re, self.n_pb, self.own, self.send = n_re, n_pb, own, send
        self.made = {}

    def get(self, kind, c):
        if (kind, c) not in self.made:
            self.made[kind, c] = None
            self.made[kind, c] = getattr(self, kind)(c)
        return self.made[kind, c]

    def gated(self, x, kind, c):
        return after(x, *[self.get(*other) for other in GATES.get((kind, c), [])])

    def received(self, c):
        out = []
        for s in range(1, self.n_re):
            message = self.gated(self.send[s - 1][c].astype(jnp.float16), "received", c)
            got = lax.ppermute(message, "re", [(i, (i + s) % self.n_re) for i in range(self.n_re)])
            out.append(got.astype(jnp.float32))
        return out

    def block(self, c):
        return add_up(self.own[c], [self.gated(got, "block", c) for got in self.get("received", c)], ADDCOST[c])

    def near(self, c):
        block = self.gated(self.get("block", c), "near", c)
        return lax.ppermute(block, "pb", [(i, i ^ 1) for i in range(self.n_pb)])

    def far(self, c):
        block = self.gated(self.get("block", c), "far", c)
        return lax.ppermute(block, "pb", [(i, i ^ 3) for i in range(self.n_pb)])

    def last(self, c):
        passed_on = relay(self.get("block", c), self.gated(self.get("far", c), "last", c), RELCOST[c])
        return lax.ppermute(passed_on, "pb", [(0, 2), (3, 1), (1, 0), (2, 3)])

    def gathered(self, c):
        block, n = self.get("block", c), self.n_pb
        if n == 4:
            return [block, self.get("near", c), self.get("far", c), self.get("last", c)]
        return [block] + [lax.ppermute(block, "pb", [(i, (i + s) % n) for i in range(n)]) for s in range(1, n)]


def body(n_re, n_pb, g_wann, phonon_phase, electron_phase):
    k_own = electron_phase.shape[1] // n_re
    p_own = g_wann.shape[1]
    cuts = [k_own * c // sum(CUTS) for c in CUTS]
    ahead = p_own // HEAD
    own, send = electron_sums(electron_phase, g_wann, n_re, [k_own], 0, ahead)
    own_rest, send_rest = electron_sums(electron_phase, g_wann, n_re, cuts, ahead, p_own - ahead)
    transfers = Transfers(n_re, n_pb, own + own_rest, [a + b for a, b in zip(send, send_rest)])
    gathered = [transfers.gathered(c) for c in range(1 + len(cuts))]
    table = phonon_phase
    q = table.shape[1]
    orders = [functools.partial(lambda i: block_order(n_pb)[i:], i) for i in (0, n_pb - 1)]
    if p_own % 128 != 0:
        table = table.reshape(2, q, n_pb, p_own)[:, :, jnp.stack(block_order(n_pb))].reshape(table.shape)
        orders = [lambda: None] * 2
    result, first = None, 0
    for c, size in enumerate(cuts):
        blocks = list(zip(gathered[0], gathered[1 + c]))
        acc, order_of = None, orders[0]
        if c == len(cuts) - 1 and p_own % 128 == 0:
            acc = phonon_main(order_of, table, blocks[:-1], first)
            blocks, order_of = blocks[-1:], orders[1]
        result = phonon_final(order_of, table, blocks, acc, result, first, k_own)
        first += size
    return result


def solution(mesh):
    return jax.shard_map(
        functools.partial(body, mesh.shape["re"], mesh.shape["pb"]),
        mesh=mesh,
        in_specs=(P(None, "pb", ("grp", "re"), "ka"), P(None, "pb", None), P()),
        out_specs=P(("grp", "re"), None, "pb", "ka"),
        check_vma=False,
    )
```

```python
import functools

import jax
import jax.numpy as jnp
from jax import lax
from jax.experimental import pallas as pl
from jax.experimental.pallas import tpu as pltpu
from jax.sharding import PartitionSpec as P

GROUP = 8
SIDE = 2
PIECES = 4
TAIL = 16
FULL = 32768.0
POWERS = (64, 32, 16, 8, 4, 2)
HEAD = (1, 4)
CUTS = (1, 3)
ADDCOST = [0, 10**10, 10**10]
GATES = {('block', 1): [('block', 0)], ('block', 2): [('near', 0), ('across', 0)], ('passed', 0): [('near', 0)], ('passed', 1): [('passed', 0)], ('received', 2, 0): [('block', 0)]}
MPIECES = (1, 1, 1)
SLICED = True
RESTGATE = ()
ECOST = 1
SPLIT = ()
LASTFINAL = False
RELCOST = [0, 0, 0]
PHON = 80
PARTS = 2
SMALL = 16 * 2**20
LARGE = 50 * 2**20
VMEM = pl.BlockSpec(memory_space=pltpu.VMEM)
HBM = pl.BlockSpec(memory_space=pltpu.HBM)


def pick(me, n, choices):
    out = choices[0]
    for i in range(1, n):
        out = jnp.where(me == i, choices[i], out)
    return out


def phase_rows(me, n_re, phase_ref):
    k_all, e_all = phase_ref.shape[1:]
    e_own, k_own = e_all // n_re, k_all // n_re
    width = GROUP * e_own
    tables = []
    for part in range(2):
        full = phase_ref[part].astype(jnp.float32)
        own = pick(me, n_re, [full[:, r * e_own : (r + 1) * e_own] for r in range(n_re)])
        tables.append(jnp.concatenate([own] * GROUP, 1))
    row = lax.broadcasted_iota(jnp.int32, (k_own * GROUP, width), 0) % GROUP
    column = lax.broadcasted_iota(jnp.int32, (k_own * GROUP, width), 1) // e_own
    spread = []
    for table in tables:
        groups = [table[r * k_own : (r + 1) * k_own] for r in range(n_re)]
        moved = [pick(me, n_re, groups[s:] + groups[:s]) for s in range(n_re)]
        spread.append([
            jnp.where(row == column, jnp.broadcast_to(m[:, None], (k_own, GROUP, width)).reshape(k_own * GROUP, width), 0.0)
            for m in moved
        ])
    cos, sin = spread
    left = jnp.concatenate([x for s in range(n_re) for x in (cos[s], sin[s])], 0)
    right = jnp.concatenate([x for s in range(n_re) for x in (-sin[s], cos[s])], 0)
    return left.astype(jnp.bfloat16), right.astype(jnp.bfloat16)


def electron_kernel(n_re, cuts, mcuts, pieces, start, phase_ref, g_ref, *refs):
    n, m = len(cuts), len(mcuts)
    own_refs, send_refs = refs[:n], refs[n : n + (n_re - 1) * m]
    g_vmem, left_ref, right_ref, sems = ([g_ref] if pieces == 0 else []) + list(refs[n + (n_re - 1) * m :])
    _, rows, e_own, b = g_vmem.shape
    size = rows // max(pieces, 1)
    copies = [
        pltpu.make_async_copy(g_ref.at[:, pl.ds(start + i * size, size)], g_vmem.at[:, pl.ds(i * size, size)], sems.at[i])
        for i in range(pieces)
    ]
    for copy in copies:
        copy.start()
    left_ref[...], right_ref[...] = phase_rows(lax.axis_index("re"), n_re, phase_ref)
    depth = GROUP * e_own
    step = SIDE * GROUP
    largest = jnp.zeros((GROUP, b), jnp.float32)
    for i in range(rows // step):
        if pieces and i * step % size == 0:
            copies[i * step // size].wait()
        groups = [pl.ds(i * step + j * GROUP, GROUP) for j in range(SIDE)]
        real = jnp.concatenate([g_vmem[0, at].reshape(depth, b) for at in groups], 1)
        imag = jnp.concatenate([g_vmem[1, at].reshape(depth, b) for at in groups], 1)
        out = jnp.dot(left_ref[...], real, preferred_element_type=jnp.float32)
        out += jnp.dot(right_ref[...], imag, preferred_element_type=jnp.float32)
        out = out.reshape(n_re, 2, -1, GROUP, SIDE * b)
        if n_re > 1:
            sent = jnp.max(jnp.abs(out[1:].reshape(-1, GROUP, SIDE * b)), 0)
            for j in range(SIDE):
                largest = jnp.maximum(largest, sent[:, j * b : (j + 1) * b])
        for j, at in enumerate(groups):
            first = 0
            for c, kept in enumerate(cuts):
                own_refs[c][:, :, at] = out[0, :, first : first + kept, :, j * b : (j + 1) * b]
                first += kept
            first = 0
            for c, kept in enumerate(mcuts):
                for s in range(1, n_re):
                    for part in range(2):
                        for k in range(kept):
                            row = (part * kept + k) * rows + i * step + j * GROUP
                            send_refs[(s - 1) * m + c][pl.ds(row, GROUP)] = out[s, part, first + k, :, j * b : (j + 1) * b]
                first += kept
    if n_re > 1:
        top = jnp.max(largest, keepdims=True)
        scale, exponent = jnp.ones((1, 1), jnp.float32), jnp.zeros((1, 1), jnp.float32)
        for bit in POWERS:
            fits = top * scale * 2.0**bit <= FULL
            scale = jnp.where(fits, scale * 2.0**bit, scale)
            exponent = jnp.where(fits, exponent + bit, exponent)
        for ref in send_refs:
            last = ref.shape[0] - TAIL
            ref[pl.ds(0, last)] = ref[pl.ds(0, last)] * scale
            ref[pl.ds(last, TAIL)] = jnp.broadcast_to(exponent, (TAIL, b))


def electron_sums(phase, g_wann, n_re, cuts, mcuts, start, rows):
    _, _, e_own, b = g_wann.shape
    k_all = phase.shape[1]
    pieces = 0 if start is None else PIECES if rows % (PIECES * SIDE * GROUP) == 0 else 1
    own = [jax.ShapeDtypeStruct((2, size, rows, b), jnp.float32) for size in cuts]
    send = [jax.ShapeDtypeStruct((2 * size * rows + TAIL, b), jnp.float32) for _ in range(n_re - 1) for size in mcuts]
    outs = pl.pallas_call(
        functools.partial(electron_kernel, n_re, cuts, mcuts, pieces, start),
        in_specs=[VMEM, HBM if pieces else VMEM],
        out_specs=[VMEM] * len(own + send),
        out_shape=own + send,
        scratch_shapes=([pltpu.VMEM((2, rows, e_own, b), g_wann.dtype)] if pieces else [])
        + [
            pltpu.VMEM((2 * k_all * GROUP, GROUP * e_own), jnp.bfloat16),
            pltpu.VMEM((2 * k_all * GROUP, GROUP * e_own), jnp.bfloat16),
            pltpu.SemaphoreType.DMA((max(pieces, 1),)),
        ],
        compiler_params=pltpu.CompilerParams(vmem_limit_bytes=LARGE if pieces else SMALL),
        cost_estimate=pl.CostEstimate(flops=ECOST * 8 * k_all * e_own * rows * b, bytes_accessed=4 * rows * e_own * b, transcendentals=0),
    )(phase, g_wann)
    return outs[: len(cuts)], [outs[len(cuts) + s * len(mcuts) : len(cuts) + (s + 1) * len(mcuts)] for s in range(n_re - 1)]


def add_kernel(pieces, own_ref, *refs):
    out_ref = refs[-1]
    _, kept, rows, _ = own_ref.shape
    totals = {(part, k): own_ref[part, k] for part in range(2) for k in range(kept)}
    for n, ref in enumerate(refs[:-1]):
        exponent = ref[pl.ds(ref.shape[0] - TAIL, 1)]
        factor = jnp.ones_like(exponent)
        for bit in POWERS:
            taken = exponent >= bit
            exponent = jnp.where(taken, exponent - bit, exponent)
            factor = jnp.where(taken, factor * 2.0**-bit, factor)
        size = kept // pieces
        for part in range(2):
            for k in range(size):
                to = part, n % pieces * size + k
                totals[to] = totals[to] + ref[pl.ds((part * size + k) * rows, rows)] * factor
    for to, total in totals.items():
        out_ref[to] = total.astype(out_ref.dtype)


def add_up(own, received, pieces, cost):
    return pl.pallas_call(
        functools.partial(add_kernel, pieces),
        in_specs=[VMEM] * (1 + len(received)),
        out_specs=VMEM,
        out_shape=jax.ShapeDtypeStruct(own.shape, jnp.bfloat16),
        compiler_params=pltpu.CompilerParams(vmem_limit_bytes=SMALL),
        cost_estimate=pl.CostEstimate(flops=cost, bytes_accessed=0, transcendentals=0),
    )(own, *received)


def origin(n, step):
    me = lax.axis_index("pb")
    return me ^ step if n == 4 else (me - step) % n


def relay_kernel(block_ref, far_ref, out_ref):
    me = lax.axis_index("pb")
    middle = (me == 1) | (me == 2)
    for c in range(2):
        out_ref[c] = jnp.where(middle, far_ref[c], block_ref[c])


def relay(block, far, cost):
    return pl.pallas_call(
        relay_kernel,
        in_specs=[VMEM, VMEM],
        out_specs=VMEM,
        out_shape=jax.ShapeDtypeStruct(block.shape, block.dtype),
        compiler_params=pltpu.CompilerParams(vmem_limit_bytes=SMALL),
        cost_estimate=pl.CostEstimate(flops=cost, bytes_accessed=0, transcendentals=0),
    )(block, far)


def after(x, *others):
    return lax.optimization_barrier((x, *others))[0] if others else x


def phonon_part(steps, n_pb, table_ref, refs, first, k, rows=slice(None)):
    total, refs = None, list(refs)
    p_own = table_ref.shape[2] // n_pb
    for n, (step, has_head) in enumerate(steps):
        if p_own % 128:
            at = pl.ds(step * p_own, p_own)
        else:
            at = pl.ds(pl.multiple_of(origin(n_pb, step) * p_own, p_own), p_own)
        head_ref = refs.pop(0) if has_head else None
        rest_ref = refs.pop(0)
        ahead, b = p_own - rest_ref.shape[2], rest_ref.shape[3]
        halves = []
        for c in range(2):
            head = head_ref[c, first + k] if has_head else jnp.zeros((ahead, b), rest_ref.dtype)
            halves.append(jnp.concatenate([head, rest_ref[c, k]], 0))
        real, imag = halves
        part = jnp.dot(table_ref[0, rows, at], jnp.concatenate([real, imag], 1), preferred_element_type=jnp.float32)
        part += jnp.dot(table_ref[1, rows, at], jnp.concatenate([-imag, real], 1), preferred_element_type=jnp.float32)
        total = part if total is None else total + part
    return total


def main_kernel(steps, n_pb, first, table_ref, *refs):
    out_ref = refs[-1]
    for k in range(out_ref.shape[0]):
        out_ref[k] = phonon_part(steps, n_pb, table_ref, refs[:-1], first, k)


def final_kernel(steps, n_pb, first, has_prior, table_ref, acc_ref, *refs):
    out_ref, staged, sems = refs[-3:]
    size, _, q, b = staged.shape
    copies = []
    for k in range(size):
        for h in range(PARTS):
            rows = pl.ds(h * (q // PARTS), q // PARTS)
            total = acc_ref[k, rows] + phonon_part(steps, n_pb, table_ref, refs[: -3 - has_prior], first, k, rows)
            staged[k, 0, rows] = total[:, :b]
            staged[k, 1, rows] = total[:, b:]
            copies.append(pltpu.make_async_copy(staged.at[k, :, rows], out_ref.at[first + k, :, rows], sems.at[k, h]))
            copies[-1].start()
    for copy in copies:
        copy.wait()


def kernel_inputs(blocks):
    steps = [(step, head is not None) for step, head, _ in blocks]
    return steps, [x for _, head, rest in blocks for x in (head, rest) if x is not None]


def phonon_main(n_pb, table, blocks, first):
    steps, flat = kernel_inputs(blocks)
    q = table.shape[1]
    _, size, rows, b = blocks[0][2].shape
    return pl.pallas_call(
        functools.partial(main_kernel, steps, n_pb, first),
        in_specs=[VMEM] * (1 + len(flat)),
        out_specs=VMEM,
        out_shape=jax.ShapeDtypeStruct((size, q, 2 * b), jnp.float32),
        compiler_params=pltpu.CompilerParams(vmem_limit_bytes=SMALL),
        cost_estimate=pl.CostEstimate(flops=PHON * q * rows * len(blocks) * b * size, bytes_accessed=0, transcendentals=0),
    )(table, *flat)


def phonon_final(n_pb, table, acc, blocks, prior, first, k_own):
    steps, flat = kernel_inputs(blocks)
    q = table.shape[1]
    _, size, rows, b = blocks[0][2].shape
    alias = [] if prior is None else [prior]
    return pl.pallas_call(
        functools.partial(final_kernel, steps, n_pb, first, len(alias)),
        in_specs=[VMEM] * (2 + len(flat)) + [HBM] * len(alias),
        out_specs=HBM,
        out_shape=jax.ShapeDtypeStruct((k_own, 2, q, b), jnp.float32),
        scratch_shapes=[pltpu.VMEM((size, 2, q, b), jnp.float32), pltpu.SemaphoreType.DMA((size, PARTS))],
        input_output_aliases={2 + len(flat): 0} if alias else {},
        compiler_params=pltpu.CompilerParams(vmem_limit_bytes=SMALL),
        cost_estimate=pl.CostEstimate(flops=PHON * q * rows * len(blocks) * b * size, bytes_accessed=size * q * b * 8, transcendentals=0),
    )(table, acc, *flat, *alias)


class Transfers:
    def __init__(self, n_re, n_pb, own, send):
        self.n_re, self.n_pb, self.own, self.send = n_re, n_pb, own, send
        self.made = {}

    def get(self, *what):
        if what not in self.made:
            self.made[what] = None
            self.made[what] = getattr(self, what[0])(*what[1:])
        return self.made[what]

    def gated(self, x, *what):
        return after(x, *[self.get(*other) for other in GATES.get(what, [])])

    def received(self, c, piece):
        out = []
        for s in range(1, self.n_re):
            message = self.gated(self.send[s - 1][c][piece].astype(jnp.float16), "received", c, piece)
            got = lax.ppermute(message, "re", [(i, (i + s) % self.n_re) for i in range(self.n_re)])
            out.append(got)
        return out

    def block(self, c):
        pieces = [self.get("received", c, i) for i in range(MPIECES[c])]
        received = [self.gated(got, "block", c).astype(jnp.float32) for several in zip(*pieces) for got in several]
        return add_up(self.own[c], received, MPIECES[c], ADDCOST[c])

    def near(self, c):
        block = self.gated(self.get("block", c), "near", c)
        return lax.ppermute(block, "pb", [(i, i ^ 1) for i in range(self.n_pb)])

    def across(self, c):
        block = self.gated(self.get("block", c), "across", c)
        pairs = [(i, i ^ 3) for i in range(self.n_pb)]
        return lax.ppermute(block, "pb", pairs[1:-1] if c in SPLIT else pairs)

    def ends(self, c):
        block = self.gated(self.get("block", c), "ends", c)
        return lax.ppermute(block, "pb", [(0, 3), (3, 0)])

    def passed(self, c):
        return relay(self.get("block", c), self.gated(self.get("across", c), "passed", c), RELCOST[c])

    def last(self, c):
        return lax.ppermute(self.get("passed", c), "pb", [(0, 2), (3, 1), (1, 0), (2, 3)])

    def shifted(self, c, s):
        return lax.ppermute(self.get("block", c), "pb", [(i, (i + s) % self.n_pb) for i in range(self.n_pb)])

    def main_blocks(self, c):
        if self.n_pb == 4:
            out = [(0, self.get("block", 0), self.get("block", c)), (1, self.get("near", 0), self.get("near", c))]
            if c in SPLIT:
                if LASTFINAL:
                    return out + [(3, None, self.get("across", c))]
                return out + [(2, self.get("last", 0), self.get("last", c)), (3, None, self.get("across", c))]
            return out + [(3, self.get("across", 0), self.get("across", c))]
        return [(s, self.shifted(0, s), self.shifted(c, s)) if s else (0, self.get("block", 0), self.get("block", c)) for s in range(self.n_pb - 1)]

    def final_blocks(self, c):
        if self.n_pb == 4:
            if c in SPLIT:
                out = [(2, self.get("last", 0), self.get("last", c))] if LASTFINAL else []
                return out + [(3, self.get("across", 0), self.get("ends", c))]
            return [(2, self.get("last", 0), self.get("last", c))]
        s = self.n_pb - 1
        return [(s, self.shifted(0, s), self.shifted(c, s))]

    def acc(self, c):
        return phonon_main(self.n_pb, self.table, self.get("main_blocks", c), self.firsts[c])


def body(n_re, n_pb, g_wann, phonon_phase, electron_phase):
    k_own = electron_phase.shape[1] // n_re
    p_own = g_wann.shape[1]
    cuts = [k_own * c // sum(CUTS) for c in CUTS]
    ahead = p_own * HEAD[0] // HEAD[1] // (2 * GROUP) * (2 * GROUP)
    if SLICED:
        own, send = electron_sums(electron_phase, g_wann[:, :ahead], n_re, [k_own], [k_own], None, ahead)
    else:
        own, send = electron_sums(electron_phase, g_wann, n_re, [k_own], [k_own], 0, ahead)
    table = phonon_phase
    if p_own % 128 != 0:
        order = jnp.stack([origin(n_pb, step) for step in range(n_pb)])
        table = table.reshape(2, -1, n_pb, p_own)[:, :, order].reshape(table.shape)
    transfers = Transfers(n_re, n_pb, own, [[a] for a in send])
    mcuts = [size // MPIECES[1 + c] for c, size in enumerate(cuts) for _ in range(MPIECES[1 + c])]
    rest = electron_sums(after(electron_phase, transfers.get(*RESTGATE) if RESTGATE else own[0]), g_wann, n_re, cuts, mcuts, ahead, p_own - ahead)
    at = [sum(MPIECES[1 : 1 + c]) for c in range(len(cuts) + 1)]
    transfers.own = own + rest[0]
    transfers.send = [[a] + [b[at[c] : at[c + 1]] for c in range(len(cuts))] for a, b in zip(send, rest[1])]
    transfers.table = table
    transfers.firsts = [None] + [sum(cuts[:c]) for c in range(len(cuts))]
    result = None
    for c in range(1, 1 + len(cuts)):
        acc = transfers.get("acc", c)
        result = phonon_final(n_pb, table, acc, transfers.get("final_blocks", c), result, transfers.firsts[c], k_own)
    return result


def solution(mesh):
    return jax.shard_map(
        functools.partial(body, mesh.shape["re"], mesh.shape["pb"]),
        mesh=mesh,
        in_specs=(P(None, "pb", ("grp", "re"), "ka"), P(None, "pb", None), P()),
        out_specs=P(("grp", "re"), None, "pb", "ka"),
        check_vma=False,
    )
```

```python
import functools

import jax
import jax.numpy as jnp
from jax import lax
from jax.experimental import pallas as pl
from jax.experimental.pallas import tpu as pltpu
from jax.sharding import PartitionSpec as P

GROUP = 8
SIDE = 2
PIECES = 4
TAIL = 16
FULL = 32768.0
POWERS = (64, 32, 16, 8, 4, 2)
HEAD = (1, 4)
CUTS = (1, 1, 2)
ADDCOST = (0, 10**10, 10**10, 10**10)
GATES = {
    ("received", 2): [("block", 0)],
    ("block", 1): [("block", 0)],
    ("block", 2): [("near", 0), ("across", 0)],
    ("block", 3): [("near", 0), ("across", 0)],
    ("passed", 1): [("passed", 0), ("block", 3)],
    ("passed", 2): [("passed", 1)],
    ("passed", 3): [("passed", 2)],
}
MCUTS = (1, 3)
PHON = 80
PARTS = 2
SMALL = 16 * 2**20
LARGE = 50 * 2**20
VMEM = pl.BlockSpec(memory_space=pltpu.VMEM)
HBM = pl.BlockSpec(memory_space=pltpu.HBM)


def pick(me, n, choices):
    out = choices[0]
    for i in range(1, n):
        out = jnp.where(me == i, choices[i], out)
    return out


def phase_rows(me, n_re, phase_ref):
    k_all, e_all = phase_ref.shape[1:]
    e_own, k_own = e_all // n_re, k_all // n_re
    width = GROUP * e_own
    tables = []
    for part in range(2):
        full = phase_ref[part].astype(jnp.float32)
        own = pick(me, n_re, [full[:, r * e_own : (r + 1) * e_own] for r in range(n_re)])
        tables.append(jnp.concatenate([own] * GROUP, 1))
    row = lax.broadcasted_iota(jnp.int32, (k_own * GROUP, width), 0) % GROUP
    column = lax.broadcasted_iota(jnp.int32, (k_own * GROUP, width), 1) // e_own
    spread = []
    for table in tables:
        groups = [table[r * k_own : (r + 1) * k_own] for r in range(n_re)]
        moved = [pick(me, n_re, groups[s:] + groups[:s]) for s in range(n_re)]
        spread.append([
            jnp.where(row == column, jnp.broadcast_to(m[:, None], (k_own, GROUP, width)).reshape(k_own * GROUP, width), 0.0)
            for m in moved
        ])
    cos, sin = spread
    left = jnp.concatenate([x for s in range(n_re) for x in (cos[s], sin[s])], 0)
    right = jnp.concatenate([x for s in range(n_re) for x in (-sin[s], cos[s])], 0)
    return left.astype(jnp.bfloat16), right.astype(jnp.bfloat16)


def electron_kernel(n_re, cuts, mcuts, pieces, start, phase_ref, g_ref, *refs):
    n, m = len(cuts), len(mcuts)
    own_refs, send_refs = refs[:n], refs[n : n + (n_re - 1) * m]
    g_vmem, left_ref, right_ref, sems = ([g_ref] if pieces == 0 else []) + list(refs[n + (n_re - 1) * m :])
    _, rows, e_own, b = g_vmem.shape
    size = rows // max(pieces, 1)
    copies = [
        pltpu.make_async_copy(g_ref.at[:, pl.ds(start + i * size, size)], g_vmem.at[:, pl.ds(i * size, size)], sems.at[i])
        for i in range(pieces)
    ]
    for copy in copies:
        copy.start()
    left_ref[...], right_ref[...] = phase_rows(lax.axis_index("re"), n_re, phase_ref)
    depth = GROUP * e_own
    step = SIDE * GROUP
    largest = jnp.zeros((GROUP, b), jnp.float32)
    for i in range(rows // step):
        if pieces and i * step % size == 0:
            copies[i * step // size].wait()
        groups = [pl.ds(i * step + j * GROUP, GROUP) for j in range(SIDE)]
        real = jnp.concatenate([g_vmem[0, at].reshape(depth, b) for at in groups], 1)
        imag = jnp.concatenate([g_vmem[1, at].reshape(depth, b) for at in groups], 1)
        out = jnp.dot(left_ref[...], real, preferred_element_type=jnp.float32)
        out += jnp.dot(right_ref[...], imag, preferred_element_type=jnp.float32)
        out = out.reshape(n_re, 2, -1, GROUP, SIDE * b)
        if n_re > 1:
            sent = jnp.max(jnp.abs(out[1:].reshape(-1, GROUP, SIDE * b)), 0)
            for j in range(SIDE):
                largest = jnp.maximum(largest, sent[:, j * b : (j + 1) * b])
        for j, at in enumerate(groups):
            first = 0
            for c, kept in enumerate(cuts):
                own_refs[c][:, :, at] = out[0, :, first : first + kept, :, j * b : (j + 1) * b]
                first += kept
            first = 0
            for c, kept in enumerate(mcuts):
                for s in range(1, n_re):
                    for part in range(2):
                        for k in range(kept):
                            row = (part * kept + k) * rows + i * step + j * GROUP
                            send_refs[(s - 1) * m + c][pl.ds(row, GROUP)] = out[s, part, first + k, :, j * b : (j + 1) * b]
                first += kept
    if n_re > 1:
        top = jnp.max(largest, keepdims=True)
        scale, exponent = jnp.ones((1, 1), jnp.float32), jnp.zeros((1, 1), jnp.float32)
        for bit in POWERS:
            fits = top * scale * 2.0**bit <= FULL
            scale = jnp.where(fits, scale * 2.0**bit, scale)
            exponent = jnp.where(fits, exponent + bit, exponent)
        for ref in send_refs:
            last = ref.shape[0] - TAIL
            ref[pl.ds(0, last)] = ref[pl.ds(0, last)] * scale
            ref[pl.ds(last, TAIL)] = jnp.broadcast_to(exponent, (TAIL, b))


def electron_sums(phase, g_wann, n_re, cuts, mcuts, start, rows):
    _, _, e_own, b = g_wann.shape
    k_all = phase.shape[1]
    pieces = 0 if start is None else PIECES if rows % (PIECES * SIDE * GROUP) == 0 else 1
    own = [jax.ShapeDtypeStruct((2, size, rows, b), jnp.float32) for size in cuts]
    send = [jax.ShapeDtypeStruct((2 * size * rows + TAIL, b), jnp.float32) for _ in range(n_re - 1) for size in mcuts]
    outs = pl.pallas_call(
        functools.partial(electron_kernel, n_re, cuts, mcuts, pieces, start),
        in_specs=[VMEM, HBM if pieces else VMEM],
        out_specs=[VMEM] * len(own + send),
        out_shape=own + send,
        scratch_shapes=([pltpu.VMEM((2, rows, e_own, b), g_wann.dtype)] if pieces else [])
        + [
            pltpu.VMEM((2 * k_all * GROUP, GROUP * e_own), jnp.bfloat16),
            pltpu.VMEM((2 * k_all * GROUP, GROUP * e_own), jnp.bfloat16),
            pltpu.SemaphoreType.DMA((max(pieces, 1),)),
        ],
        compiler_params=pltpu.CompilerParams(vmem_limit_bytes=LARGE if pieces else SMALL),
        cost_estimate=pl.CostEstimate(flops=8 * k_all * e_own * rows * b, bytes_accessed=4 * rows * e_own * b, transcendentals=0),
    )(phase, g_wann)
    return outs[: len(cuts)], [outs[len(cuts) + s * len(mcuts) : len(cuts) + (s + 1) * len(mcuts)] for s in range(n_re - 1)]


def add_kernel(first, own_ref, *refs):
    out_ref = refs[-1]
    _, kept, rows, _ = own_ref.shape
    totals = {(part, k): own_ref[part, k] for part in range(2) for k in range(kept)}
    for ref in refs[:-1]:
        exponent = ref[pl.ds(ref.shape[0] - TAIL, 1)]
        factor = jnp.ones_like(exponent)
        for bit in POWERS:
            taken = exponent >= bit
            exponent = jnp.where(taken, exponent - bit, exponent)
            factor = jnp.where(taken, factor * 2.0**-bit, factor)
        carried = (ref.shape[0] - TAIL) // (2 * rows)
        for part, k in totals:
            at = pl.ds((part * carried + first + k) * rows, rows)
            totals[part, k] = totals[part, k] + ref[at] * factor
    for to, total in totals.items():
        out_ref[to] = total.astype(out_ref.dtype)


def add_up(own, received, first, cost):
    return pl.pallas_call(
        functools.partial(add_kernel, first),
        in_specs=[VMEM] * (1 + len(received)),
        out_specs=VMEM,
        out_shape=jax.ShapeDtypeStruct(own.shape, jnp.bfloat16),
        compiler_params=pltpu.CompilerParams(vmem_limit_bytes=SMALL),
        cost_estimate=pl.CostEstimate(flops=cost, bytes_accessed=0, transcendentals=0),
    )(own, *received)


def origin(n, step):
    me = lax.axis_index("pb")
    return me ^ step if n == 4 else (me - step) % n


def relay_kernel(block_ref, far_ref, out_ref):
    me = lax.axis_index("pb")
    middle = (me == 1) | (me == 2)
    for c in range(2):
        out_ref[c] = jnp.where(middle, far_ref[c], block_ref[c])


def relay(block, far):
    return pl.pallas_call(
        relay_kernel,
        in_specs=[VMEM, VMEM],
        out_specs=VMEM,
        out_shape=jax.ShapeDtypeStruct(block.shape, block.dtype),
        compiler_params=pltpu.CompilerParams(vmem_limit_bytes=SMALL),
        cost_estimate=pl.CostEstimate(flops=0, bytes_accessed=0, transcendentals=0),
    )(block, far)


def after(x, *others):
    return lax.optimization_barrier((x, *others))[0] if others else x


def phonon_part(steps, n_pb, table_ref, refs, first, k, rows=slice(None)):
    total = None
    p_own = table_ref.shape[2] // n_pb
    for step, head_ref, rest_ref in zip(steps, refs[::2], refs[1::2]):
        if p_own % 128:
            at = pl.ds(step * p_own, p_own)
        else:
            at = pl.ds(pl.multiple_of(origin(n_pb, step) * p_own, p_own), p_own)
        real, imag = [jnp.concatenate([head_ref[c, first + k], rest_ref[c, k]], 0) for c in range(2)]
        part = jnp.dot(table_ref[0, rows, at], jnp.concatenate([real, imag], 1), preferred_element_type=jnp.float32)
        part += jnp.dot(table_ref[1, rows, at], jnp.concatenate([-imag, real], 1), preferred_element_type=jnp.float32)
        total = part if total is None else total + part
    return total


def main_kernel(steps, n_pb, first, table_ref, *refs):
    out_ref = refs[-1]
    for k in range(out_ref.shape[0]):
        out_ref[k] = phonon_part(steps, n_pb, table_ref, refs[:-1], first, k)


def final_kernel(steps, n_pb, first, has_prior, table_ref, acc_ref, *refs):
    out_ref, staged, sems = refs[-3:]
    size, _, q, b = staged.shape
    copies = []
    for k in range(size):
        for h in range(PARTS):
            rows = pl.ds(h * (q // PARTS), q // PARTS)
            total = acc_ref[k, rows] + phonon_part(steps, n_pb, table_ref, refs[: -3 - has_prior], first, k, rows)
            staged[k, 0, rows] = total[:, :b]
            staged[k, 1, rows] = total[:, b:]
            copies.append(pltpu.make_async_copy(staged.at[k, :, rows], out_ref.at[first + k, :, rows], sems.at[k, h]))
            copies[-1].start()
    for copy in copies:
        copy.wait()


def kernel_inputs(blocks):
    return [step for step, _, _ in blocks], [x for _, head, rest in blocks for x in (head, rest)]


def phonon_main(n_pb, table, blocks, first):
    steps, flat = kernel_inputs(blocks)
    q = table.shape[1]
    _, size, rows, b = blocks[0][2].shape
    return pl.pallas_call(
        functools.partial(main_kernel, steps, n_pb, first),
        in_specs=[VMEM] * (1 + len(flat)),
        out_specs=VMEM,
        out_shape=jax.ShapeDtypeStruct((size, q, 2 * b), jnp.float32),
        compiler_params=pltpu.CompilerParams(vmem_limit_bytes=SMALL),
        cost_estimate=pl.CostEstimate(flops=PHON * q * rows * len(blocks) * b * size, bytes_accessed=0, transcendentals=0),
    )(table, *flat)


def phonon_final(n_pb, table, acc, blocks, prior, first, k_own):
    steps, flat = kernel_inputs(blocks)
    q = table.shape[1]
    _, size, rows, b = blocks[0][2].shape
    alias = [] if prior is None else [prior]
    return pl.pallas_call(
        functools.partial(final_kernel, steps, n_pb, first, len(alias)),
        in_specs=[VMEM] * (2 + len(flat)) + [HBM] * len(alias),
        out_specs=HBM,
        out_shape=jax.ShapeDtypeStruct((k_own, 2, q, b), jnp.float32),
        scratch_shapes=[pltpu.VMEM((size, 2, q, b), jnp.float32), pltpu.SemaphoreType.DMA((size, PARTS))],
        input_output_aliases={2 + len(flat): 0} if alias else {},
        compiler_params=pltpu.CompilerParams(vmem_limit_bytes=SMALL),
        cost_estimate=pl.CostEstimate(flops=PHON * q * rows * len(blocks) * b * size, bytes_accessed=size * q * b * 8, transcendentals=0),
    )(table, acc, *flat, *alias)


class Transfers:
    def __init__(self, n_re, n_pb, own, send):
        self.n_re, self.n_pb, self.own, self.send = n_re, n_pb, own, send
        self.made = {}
        self.steps = (0, 1, 3, 2) if n_pb == 4 else tuple(range(n_pb))

    def get(self, *what):
        if what not in self.made:
            self.made[what] = None
            self.made[what] = getattr(self, what[0])(*what[1:])
        return self.made[what]

    def gated(self, x, *what):
        gates = GATES.get(what, []) if self.n_pb == 4 else []
        return after(x, *[self.get(*other) for other in gates])

    def received(self, m):
        out = []
        for s in range(1, self.n_re):
            message = self.gated(self.send[s - 1][m].astype(jnp.float16), "received", m)
            out.append(lax.ppermute(message, "re", [(i, (i + s) % self.n_re) for i in range(self.n_re)]))
        return out

    def block(self, c):
        m, first = self.carrier[c]
        received = [self.gated(got, "block", c).astype(jnp.float32) for got in self.get("received", m)]
        return add_up(self.own[c], received, first, ADDCOST[c])

    def near(self, c):
        block = self.gated(self.get("block", c), "near", c)
        return lax.ppermute(block, "pb", [(i, i ^ 1) for i in range(self.n_pb)])

    def across(self, c):
        block = self.gated(self.get("block", c), "across", c)
        return lax.ppermute(block, "pb", [(i, i ^ 3) for i in range(self.n_pb)])

    def passed(self, c):
        return relay(self.get("block", c), self.gated(self.get("across", c), "passed", c))

    def last(self, c):
        return lax.ppermute(self.get("passed", c), "pb", [(0, 2), (3, 1), (1, 0), (2, 3)])

    def shifted(self, c, s):
        return lax.ppermute(self.get("block", c), "pb", [(i, (i + s) % self.n_pb) for i in range(self.n_pb)])

    def step(self, c, s):
        if s == 0:
            return self.get("block", c)
        if self.n_pb == 4:
            return self.get({1: "near", 2: "last", 3: "across"}[s], c)
        return self.get("shifted", c, s)

    def blocks(self, c, steps):
        return [(s, self.step(0, s), self.step(c, s)) for s in steps]

    def acc(self, c):
        return phonon_main(self.n_pb, self.table, self.blocks(c, self.steps[:-1]), self.firsts[c])


def body(n_re, n_pb, g_wann, phonon_phase, electron_phase):
    k_own = electron_phase.shape[1] // n_re
    p_own = g_wann.shape[1]
    cuts = [k_own * c // sum(CUTS) for c in CUTS]
    ahead = p_own * HEAD[0] // HEAD[1] // (2 * GROUP) * (2 * GROUP)
    own, send = electron_sums(electron_phase, g_wann[:, :ahead], n_re, [k_own], [k_own], None, ahead)
    table = phonon_phase
    if p_own % 128 != 0:
        order = jnp.stack([origin(n_pb, step) for step in range(n_pb)])
        table = table.reshape(2, -1, n_pb, p_own)[:, :, order].reshape(table.shape)
    transfers = Transfers(n_re, n_pb, own, [list(a) for a in send])
    transfers.carrier = [(0, 0)]
    mcuts = [k_own * m // sum(MCUTS) for m in MCUTS]
    for c in range(len(cuts)):
        first = sum(cuts[:c])
        m = max(m for m in range(len(mcuts)) if sum(mcuts[:m]) <= first)
        transfers.carrier.append((1 + m, first - sum(mcuts[:m])))
    rest = electron_sums(after(electron_phase, own[0]), g_wann, n_re, cuts, mcuts, ahead, p_own - ahead)
    transfers.own = list(own) + list(rest[0])
    transfers.send = [list(a) + list(b) for a, b in zip(send, rest[1])]
    transfers.table = table
    transfers.firsts = [None] + [sum(cuts[:c]) for c in range(len(cuts))]
    result = None
    for c in range(1, 1 + len(cuts)):
        acc = transfers.get("acc", c)
        result = phonon_final(n_pb, table, acc, transfers.blocks(c, transfers.steps[-1:]), result, transfers.firsts[c], k_own)
    return result


def solution(mesh):
    return jax.shard_map(
        functools.partial(body, mesh.shape["re"], mesh.shape["pb"]),
        mesh=mesh,
        in_specs=(P(None, "pb", ("grp", "re"), "ka"), P(None, "pb", None), P()),
        out_specs=P(("grp", "re"), None, "pb", "ka"),
        check_vma=False,
    )
```

```python
import functools

import jax
import jax.numpy as jnp
from jax import lax
from jax.experimental import pallas as pl
from jax.experimental.pallas import tpu as pltpu
from jax.sharding import PartitionSpec as P

GROUP = 8
SIDE = 2
PIECES = 4
TAIL = 16
FULL = 32768.0
POWERS = (64, 32, 16, 8, 4, 2)
HEAD = (1, 4)
CUTS = (1, 1, 2)
ADDCOST = (0, 10**10, 10**10, 10**10)
GATES = {
    ("block", 1): [("block", 0)],
    ("block", 2): [("near", 0), ("across", 0)],
    ("block", 3): [("near", 0), ("across", 0)],
    ("passed", 0): [("near", 0)],
    ("passed", 1): [("passed", 0), ("block", 3)],
    ("passed", 2): [("passed", 1)],
    ("passed", 3): [("passed", 2)],
    ("received", 2): [("block", 0)],
}
MCUTS = (1, 3)
PHON = 80
PARTS = 2
SMALL = 16 * 2**20
LARGE = 50 * 2**20
VMEM = pl.BlockSpec(memory_space=pltpu.VMEM)
HBM = pl.BlockSpec(memory_space=pltpu.HBM)


def pick(me, n, choices):
    out = choices[0]
    for i in range(1, n):
        out = jnp.where(me == i, choices[i], out)
    return out


def phase_rows(me, n_re, phase_ref):
    k_all, e_all = phase_ref.shape[1:]
    e_own, k_own = e_all // n_re, k_all // n_re
    width = GROUP * e_own
    tables = []
    for part in range(2):
        full = phase_ref[part].astype(jnp.float32)
        own = pick(me, n_re, [full[:, r * e_own : (r + 1) * e_own] for r in range(n_re)])
        tables.append(jnp.concatenate([own] * GROUP, 1))
    row = lax.broadcasted_iota(jnp.int32, (k_own * GROUP, width), 0) % GROUP
    column = lax.broadcasted_iota(jnp.int32, (k_own * GROUP, width), 1) // e_own
    spread = []
    for table in tables:
        groups = [table[r * k_own : (r + 1) * k_own] for r in range(n_re)]
        moved = [pick(me, n_re, groups[s:] + groups[:s]) for s in range(n_re)]
        spread.append([
            jnp.where(row == column, jnp.broadcast_to(m[:, None], (k_own, GROUP, width)).reshape(k_own * GROUP, width), 0.0)
            for m in moved
        ])
    cos, sin = spread
    left = jnp.concatenate([x for s in range(n_re) for x in (cos[s], sin[s])], 0)
    right = jnp.concatenate([x for s in range(n_re) for x in (-sin[s], cos[s])], 0)
    return left.astype(jnp.bfloat16), right.astype(jnp.bfloat16)


def electron_kernel(n_re, cuts, mcuts, pieces, start, phase_ref, g_ref, *refs):
    n, m = len(cuts), len(mcuts)
    own_refs, send_refs = refs[:n], refs[n : n + (n_re - 1) * m]
    g_vmem, left_ref, right_ref, sems = ([g_ref] if pieces == 0 else []) + list(refs[n + (n_re - 1) * m :])
    _, rows, e_own, b = g_vmem.shape
    size = rows // max(pieces, 1)
    copies = [
        pltpu.make_async_copy(g_ref.at[:, pl.ds(start + i * size, size)], g_vmem.at[:, pl.ds(i * size, size)], sems.at[i])
        for i in range(pieces)
    ]
    for copy in copies:
        copy.start()
    left_ref[...], right_ref[...] = phase_rows(lax.axis_index("re"), n_re, phase_ref)
    depth = GROUP * e_own
    step = SIDE * GROUP
    largest = jnp.zeros((GROUP, b), jnp.float32)
    for i in range(rows // step):
        if pieces and i * step % size == 0:
            copies[i * step // size].wait()
        groups = [pl.ds(i * step + j * GROUP, GROUP) for j in range(SIDE)]
        real = jnp.concatenate([g_vmem[0, at].reshape(depth, b) for at in groups], 1)
        imag = jnp.concatenate([g_vmem[1, at].reshape(depth, b) for at in groups], 1)
        out = jnp.dot(left_ref[...], real, preferred_element_type=jnp.float32)
        out += jnp.dot(right_ref[...], imag, preferred_element_type=jnp.float32)
        out = out.reshape(n_re, 2, -1, GROUP, SIDE * b)
        if n_re > 1:
            sent = jnp.max(jnp.abs(out[1:].reshape(-1, GROUP, SIDE * b)), 0)
            for j in range(SIDE):
                largest = jnp.maximum(largest, sent[:, j * b : (j + 1) * b])
        for j, at in enumerate(groups):
            first = 0
            for c, kept in enumerate(cuts):
                own_refs[c][:, :, at] = out[0, :, first : first + kept, :, j * b : (j + 1) * b]
                first += kept
            first = 0
            for c, kept in enumerate(mcuts):
                for s in range(1, n_re):
                    for part in range(2):
                        for k in range(kept):
                            row = (part * kept + k) * rows + i * step + j * GROUP
                            send_refs[(s - 1) * m + c][pl.ds(row, GROUP)] = out[s, part, first + k, :, j * b : (j + 1) * b]
                first += kept
    if n_re > 1:
        top = jnp.max(largest, keepdims=True)
        scale, exponent = jnp.ones((1, 1), jnp.float32), jnp.zeros((1, 1), jnp.float32)
        for bit in POWERS:
            fits = top * scale * 2.0**bit <= FULL
            scale = jnp.where(fits, scale * 2.0**bit, scale)
            exponent = jnp.where(fits, exponent + bit, exponent)
        for ref in send_refs:
            last = ref.shape[0] - TAIL
            ref[pl.ds(0, last)] = ref[pl.ds(0, last)] * scale
            ref[pl.ds(last, TAIL)] = jnp.broadcast_to(exponent, (TAIL, b))


def electron_sums(phase, g_wann, n_re, cuts, mcuts, start, rows):
    _, _, e_own, b = g_wann.shape
    k_all = phase.shape[1]
    pieces = 0 if start is None else PIECES if rows % (PIECES * SIDE * GROUP) == 0 else 1
    own = [jax.ShapeDtypeStruct((2, size, rows, b), jnp.float32) for size in cuts]
    send = [jax.ShapeDtypeStruct((2 * size * rows + TAIL, b), jnp.float32) for _ in range(n_re - 1) for size in mcuts]
    outs = pl.pallas_call(
        functools.partial(electron_kernel, n_re, cuts, mcuts, pieces, start),
        in_specs=[VMEM, HBM if pieces else VMEM],
        out_specs=[VMEM] * len(own + send),
        out_shape=own + send,
        scratch_shapes=([pltpu.VMEM((2, rows, e_own, b), g_wann.dtype)] if pieces else [])
        + [
            pltpu.VMEM((2 * k_all * GROUP, GROUP * e_own), jnp.bfloat16),
            pltpu.VMEM((2 * k_all * GROUP, GROUP * e_own), jnp.bfloat16),
            pltpu.SemaphoreType.DMA((max(pieces, 1),)),
        ],
        compiler_params=pltpu.CompilerParams(vmem_limit_bytes=LARGE if pieces else SMALL),
        cost_estimate=pl.CostEstimate(flops=8 * k_all * e_own * rows * b, bytes_accessed=4 * rows * e_own * b, transcendentals=0),
    )(phase, g_wann)
    return outs[: len(cuts)], [outs[len(cuts) + s * len(mcuts) : len(cuts) + (s + 1) * len(mcuts)] for s in range(n_re - 1)]


def add_kernel(first, own_ref, *refs):
    out_ref = refs[-1]
    _, kept, rows, _ = own_ref.shape
    totals = {(part, k): own_ref[part, k] for part in range(2) for k in range(kept)}
    for ref in refs[:-1]:
        exponent = ref[pl.ds(ref.shape[0] - TAIL, 1)]
        factor = jnp.ones_like(exponent)
        for bit in POWERS:
            taken = exponent >= bit
            exponent = jnp.where(taken, exponent - bit, exponent)
            factor = jnp.where(taken, factor * 2.0**-bit, factor)
        carried = (ref.shape[0] - TAIL) // (2 * rows)
        for part, k in totals:
            at = pl.ds((part * carried + first + k) * rows, rows)
            totals[part, k] = totals[part, k] + ref[at] * factor
    for to, total in totals.items():
        out_ref[to] = total.astype(out_ref.dtype)


def add_up(own, received, first, cost):
    return pl.pallas_call(
        functools.partial(add_kernel, first),
        in_specs=[VMEM] * (1 + len(received)),
        out_specs=VMEM,
        out_shape=jax.ShapeDtypeStruct(own.shape, jnp.bfloat16),
        compiler_params=pltpu.CompilerParams(vmem_limit_bytes=SMALL),
        cost_estimate=pl.CostEstimate(flops=cost, bytes_accessed=0, transcendentals=0),
    )(own, *received)


def origin(n, step):
    me = lax.axis_index("pb")
    return me ^ step if n == 4 else (me - step) % n


def after(x, *others):
    return lax.optimization_barrier((x, *others))[0] if others else x


def phonon_part(steps, n_pb, table_ref, refs, first, k, rows=slice(None)):
    total = None
    p_own = table_ref.shape[2] // n_pb
    for step, head_ref, rest_ref in zip(steps, refs[::2], refs[1::2]):
        if p_own % 128:
            at = pl.ds(step * p_own, p_own)
        else:
            at = pl.ds(pl.multiple_of(origin(n_pb, step) * p_own, p_own), p_own)
        real, imag = [jnp.concatenate([head_ref[c, first + k], rest_ref[c, k]], 0) for c in range(2)]
        part = jnp.dot(table_ref[0, rows, at], jnp.concatenate([real, imag], 1), preferred_element_type=jnp.float32)
        part += jnp.dot(table_ref[1, rows, at], jnp.concatenate([-imag, real], 1), preferred_element_type=jnp.float32)
        total = part if total is None else total + part
    return total


def main_kernel(steps, n_pb, first, table_ref, *refs):
    out_ref = refs[-1]
    for k in range(out_ref.shape[0]):
        out_ref[k] = phonon_part(steps, n_pb, table_ref, refs[:-1], first, k)


def final_kernel(steps, n_pb, first, has_prior, table_ref, acc_ref, *refs):
    out_ref, staged, sems = refs[-3:]
    size, _, q, b = staged.shape
    copies = []
    for k in range(size):
        for h in range(PARTS):
            rows = pl.ds(h * (q // PARTS), q // PARTS)
            total = acc_ref[k, rows] + phonon_part(steps, n_pb, table_ref, refs[: -3 - has_prior], first, k, rows)
            staged[k, 0, rows] = total[:, :b]
            staged[k, 1, rows] = total[:, b:]
            copies.append(pltpu.make_async_copy(staged.at[k, :, rows], out_ref.at[first + k, :, rows], sems.at[k, h]))
            copies[-1].start()
    for copy in copies:
        copy.wait()


def kernel_inputs(blocks):
    return [step for step, _, _ in blocks], [x for _, head, rest in blocks for x in (head, rest)]


def phonon_main(n_pb, table, blocks, first):
    steps, flat = kernel_inputs(blocks)
    q = table.shape[1]
    _, size, rows, b = blocks[0][2].shape
    return pl.pallas_call(
        functools.partial(main_kernel, steps, n_pb, first),
        in_specs=[VMEM] * (1 + len(flat)),
        out_specs=VMEM,
        out_shape=jax.ShapeDtypeStruct((size, q, 2 * b), jnp.float32),
        compiler_params=pltpu.CompilerParams(vmem_limit_bytes=SMALL),
        cost_estimate=pl.CostEstimate(flops=PHON * q * rows * len(blocks) * b * size, bytes_accessed=0, transcendentals=0),
    )(table, *flat)


def phonon_final(n_pb, table, acc, blocks, prior, first, k_own):
    steps, flat = kernel_inputs(blocks)
    q = table.shape[1]
    _, size, rows, b = blocks[0][2].shape
    alias = [] if prior is None else [prior]
    return pl.pallas_call(
        functools.partial(final_kernel, steps, n_pb, first, len(alias)),
        in_specs=[VMEM] * (2 + len(flat)) + [HBM] * len(alias),
        out_specs=HBM,
        out_shape=jax.ShapeDtypeStruct((k_own, 2, q, b), jnp.float32),
        scratch_shapes=[pltpu.VMEM((size, 2, q, b), jnp.float32), pltpu.SemaphoreType.DMA((size, PARTS))],
        input_output_aliases={2 + len(flat): 0} if alias else {},
        compiler_params=pltpu.CompilerParams(vmem_limit_bytes=SMALL),
        cost_estimate=pl.CostEstimate(flops=PHON * q * rows * len(blocks) * b * size, bytes_accessed=size * q * b * 8, transcendentals=0),
    )(table, acc, *flat, *alias)


class Transfers:
    def __init__(self, n_re, n_pb, own, send):
        self.n_re, self.n_pb, self.own, self.send = n_re, n_pb, own, send
        self.made = {}
        self.steps = tuple(range(n_pb))

    def get(self, *what):
        if what not in self.made:
            self.made[what] = None
            self.made[what] = getattr(self, what[0])(*what[1:])
        return self.made[what]

    def gated(self, x, *what):
        gates = GATES.get(what, []) if self.n_pb == 4 else []
        return after(x, *[self.get(*other) for other in gates])

    def received(self, m):
        out = []
        for s in range(1, self.n_re):
            message = self.gated(self.send[s - 1][m].astype(jnp.float16), "received", m)
            out.append(lax.ppermute(message, "re", [(i, (i + s) % self.n_re) for i in range(self.n_re)]))
        return out

    def block(self, c):
        m, first = self.carrier[c]
        received = [self.gated(got, "block", c).astype(jnp.float32) for got in self.get("received", m)]
        return add_up(self.own[c], received, first, ADDCOST[c])

    def near(self, c):
        block = self.gated(self.get("block", c), "near", c)
        return lax.ppermute(block, "pb", [(i, i ^ 1) for i in range(self.n_pb)])

    def across(self, c):
        block = self.gated(self.get("block", c), "across", c)
        return lax.ppermute(block, "pb", [(i, i ^ 2) for i in range(self.n_pb)])

    def passed(self, c):
        return self.gated(self.get("across", c), "passed", c)

    def last(self, c):
        return lax.ppermute(self.get("passed", c), "pb", [(i, i ^ 1) for i in range(self.n_pb)])

    def shifted(self, c, s):
        return lax.ppermute(self.get("block", c), "pb", [(i, (i + s) % self.n_pb) for i in range(self.n_pb)])

    def step(self, c, s):
        if s == 0:
            return self.get("block", c)
        if self.n_pb == 4:
            return self.get({1: "near", 2: "across", 3: "last"}[s], c)
        return self.get("shifted", c, s)

    def blocks(self, c, steps):
        return [(s, self.step(0, s), self.step(c, s)) for s in steps]

    def acc(self, c):
        return phonon_main(self.n_pb, self.table, self.blocks(c, self.steps[:-1]), self.firsts[c])


def body(n_re, n_pb, g_wann, phonon_phase, electron_phase):
    k_own = electron_phase.shape[1] // n_re
    p_own = g_wann.shape[1]
    cuts = [k_own * c // sum(CUTS) for c in CUTS]
    ahead = p_own * HEAD[0] // HEAD[1] // (2 * GROUP) * (2 * GROUP)
    own, send = electron_sums(electron_phase, g_wann[:, :ahead], n_re, [k_own], [k_own], None, ahead)
    table = phonon_phase
    if p_own % 128 != 0:
        order = jnp.stack([origin(n_pb, step) for step in range(n_pb)])
        table = table.reshape(2, -1, n_pb, p_own)[:, :, order].reshape(table.shape)
    transfers = Transfers(n_re, n_pb, own, [list(a) for a in send])
    transfers.carrier = [(0, 0)]
    mcuts = [k_own * m // sum(MCUTS) for m in MCUTS]
    for c in range(len(cuts)):
        first = sum(cuts[:c])
        m = max(m for m in range(len(mcuts)) if sum(mcuts[:m]) <= first)
        transfers.carrier.append((1 + m, first - sum(mcuts[:m])))
    rest = electron_sums(after(electron_phase, own[0]), g_wann, n_re, cuts, mcuts, ahead, p_own - ahead)
    transfers.own = list(own) + list(rest[0])
    transfers.send = [list(a) + list(b) for a, b in zip(send, rest[1])]
    transfers.table = table
    transfers.firsts = [None] + [sum(cuts[:c]) for c in range(len(cuts))]
    result = None
    for c in range(1, 1 + len(cuts)):
        acc = transfers.get("acc", c)
        result = phonon_final(n_pb, table, acc, transfers.blocks(c, transfers.steps[-1:]), result, transfers.firsts[c], k_own)
    return result


def solution(mesh):
    return jax.shard_map(
        functools.partial(body, mesh.shape["re"], mesh.shape["pb"]),
        mesh=mesh,
        in_specs=(P(None, "pb", ("grp", "re"), "ka"), P(None, "pb", None), P()),
        out_specs=P(("grp", "re"), None, "pb", "ka"),
        check_vma=False,
    )
```

```python
import functools

import jax
import jax.numpy as jnp
from jax import lax
from jax.experimental import pallas as pl
from jax.experimental.pallas import tpu as pltpu
from jax.sharding import PartitionSpec as P

GROUP = 8
SIDE = 2
PIECES = 4
TAIL = 16
FULL = 32768.0
POWERS = (64, 32, 16, 8, 4, 2)
HEAD = (1, 4)
CUTS = (1, 1, 2)
ADDCOST = (0, 10**10, 10**10, 10**10)
GATES = {
    ("block", 1): [("block", 0)],
    ("block", 2): [("near", 0), ("across", 0)],
    ("block", 3): [("near", 0), ("across", 0)],
    ("passed", 0): [("near", 0)],
    ("passed", 1): [("passed", 0), ("block", 3), ("near", 1)],
    ("passed", 2): [("passed", 1), ("near", 2)],
    ("passed", 3): [("passed", 2)],
    ("received", 2): [("block", 0)],
}
MCUTS = (1, 3)
PHON = 80
PARTS = 2
SMALL = 16 * 2**20
LARGE = 50 * 2**20
VMEM = pl.BlockSpec(memory_space=pltpu.VMEM)
HBM = pl.BlockSpec(memory_space=pltpu.HBM)


def pick(me, n, choices):
    out = choices[0]
    for i in range(1, n):
        out = jnp.where(me == i, choices[i], out)
    return out


def phase_rows(me, n_re, phase_ref):
    k_all, e_all = phase_ref.shape[1:]
    e_own, k_own = e_all // n_re, k_all // n_re
    width = GROUP * e_own
    tables = []
    for part in range(2):
        full = phase_ref[part].astype(jnp.float32)
        own = pick(me, n_re, [full[:, r * e_own : (r + 1) * e_own] for r in range(n_re)])
        tables.append(jnp.concatenate([own] * GROUP, 1))
    row = lax.broadcasted_iota(jnp.int32, (k_own * GROUP, width), 0) % GROUP
    column = lax.broadcasted_iota(jnp.int32, (k_own * GROUP, width), 1) // e_own
    spread = []
    for table in tables:
        groups = [table[r * k_own : (r + 1) * k_own] for r in range(n_re)]
        moved = [pick(me, n_re, groups[s:] + groups[:s]) for s in range(n_re)]
        spread.append([
            jnp.where(row == column, jnp.broadcast_to(m[:, None], (k_own, GROUP, width)).reshape(k_own * GROUP, width), 0.0)
            for m in moved
        ])
    cos, sin = spread
    left = jnp.concatenate([x for s in range(n_re) for x in (cos[s], sin[s])], 0)
    right = jnp.concatenate([x for s in range(n_re) for x in (-sin[s], cos[s])], 0)
    return left.astype(jnp.bfloat16), right.astype(jnp.bfloat16)


def electron_kernel(n_re, cuts, mcuts, pieces, start, phase_ref, g_ref, *refs):
    n, m = len(cuts), len(mcuts)
    own_refs, send_refs = refs[:n], refs[n : n + (n_re - 1) * m]
    g_vmem, left_ref, right_ref, sems = ([g_ref] if pieces == 0 else []) + list(refs[n + (n_re - 1) * m :])
    _, rows, e_own, b = g_vmem.shape
    size = rows // max(pieces, 1)
    copies = [
        pltpu.make_async_copy(g_ref.at[:, pl.ds(start + i * size, size)], g_vmem.at[:, pl.ds(i * size, size)], sems.at[i])
        for i in range(pieces)
    ]
    for copy in copies:
        copy.start()
    left_ref[...], right_ref[...] = phase_rows(lax.axis_index("re"), n_re, phase_ref)
    depth = GROUP * e_own
    step = SIDE * GROUP
    largest = jnp.zeros((GROUP, b), jnp.float32)
    for i in range(rows // step):
        if pieces and i * step % size == 0:
            copies[i * step // size].wait()
        groups = [pl.ds(i * step + j * GROUP, GROUP) for j in range(SIDE)]
        real = jnp.concatenate([g_vmem[0, at].reshape(depth, b) for at in groups], 1)
        imag = jnp.concatenate([g_vmem[1, at].reshape(depth, b) for at in groups], 1)
        out = jnp.dot(left_ref[...], real, preferred_element_type=jnp.float32)
        out += jnp.dot(right_ref[...], imag, preferred_element_type=jnp.float32)
        out = out.reshape(n_re, 2, -1, GROUP, SIDE * b)
        if n_re > 1:
            sent = jnp.max(jnp.abs(out[1:].reshape(-1, GROUP, SIDE * b)), 0)
            for j in range(SIDE):
                largest = jnp.maximum(largest, sent[:, j * b : (j + 1) * b])
        for j, at in enumerate(groups):
            first = 0
            for c, kept in enumerate(cuts):
                own_refs[c][:, :, at] = out[0, :, first : first + kept, :, j * b : (j + 1) * b]
                first += kept
            first = 0
            for c, kept in enumerate(mcuts):
                for s in range(1, n_re):
                    for part in range(2):
                        for k in range(kept):
                            row = (part * kept + k) * rows + i * step + j * GROUP
                            send_refs[(s - 1) * m + c][pl.ds(row, GROUP)] = out[s, part, first + k, :, j * b : (j + 1) * b]
                first += kept
    if n_re > 1:
        top = jnp.max(largest, keepdims=True)
        scale, exponent = jnp.ones((1, 1), jnp.float32), jnp.zeros((1, 1), jnp.float32)
        for bit in POWERS:
            fits = top * scale * 2.0**bit <= FULL
            scale = jnp.where(fits, scale * 2.0**bit, scale)
            exponent = jnp.where(fits, exponent + bit, exponent)
        for ref in send_refs:
            last = ref.shape[0] - TAIL
            ref[pl.ds(0, last)] = ref[pl.ds(0, last)] * scale
            ref[pl.ds(last, TAIL)] = jnp.broadcast_to(exponent, (TAIL, b))


def electron_sums(phase, g_wann, n_re, cuts, mcuts, start, rows):
    _, _, e_own, b = g_wann.shape
    k_all = phase.shape[1]
    pieces = 0 if start is None else PIECES if rows % (PIECES * SIDE * GROUP) == 0 else 1
    own = [jax.ShapeDtypeStruct((2, size, rows, b), jnp.float32) for size in cuts]
    send = [jax.ShapeDtypeStruct((2 * size * rows + TAIL, b), jnp.float32) for _ in range(n_re - 1) for size in mcuts]
    outs = pl.pallas_call(
        functools.partial(electron_kernel, n_re, cuts, mcuts, pieces, start),
        in_specs=[VMEM, HBM if pieces else VMEM],
        out_specs=[VMEM] * len(own + send),
        out_shape=own + send,
        scratch_shapes=([pltpu.VMEM((2, rows, e_own, b), g_wann.dtype)] if pieces else [])
        + [
            pltpu.VMEM((2 * k_all * GROUP, GROUP * e_own), jnp.bfloat16),
            pltpu.VMEM((2 * k_all * GROUP, GROUP * e_own), jnp.bfloat16),
            pltpu.SemaphoreType.DMA((max(pieces, 1),)),
        ],
        compiler_params=pltpu.CompilerParams(vmem_limit_bytes=LARGE if pieces else SMALL),
        cost_estimate=pl.CostEstimate(flops=8 * k_all * e_own * rows * b, bytes_accessed=4 * rows * e_own * b, transcendentals=0),
    )(phase, g_wann)
    return outs[: len(cuts)], [outs[len(cuts) + s * len(mcuts) : len(cuts) + (s + 1) * len(mcuts)] for s in range(n_re - 1)]


def add_kernel(first, own_ref, *refs):
    out_ref = refs[-1]
    _, kept, rows, _ = own_ref.shape
    totals = {(part, k): own_ref[part, k] for part in range(2) for k in range(kept)}
    for ref in refs[:-1]:
        exponent = ref[pl.ds(ref.shape[0] - TAIL, 1)]
        factor = jnp.ones_like(exponent)
        for bit in POWERS:
            taken = exponent >= bit
            exponent = jnp.where(taken, exponent - bit, exponent)
            factor = jnp.where(taken, factor * 2.0**-bit, factor)
        carried = (ref.shape[0] - TAIL) // (2 * rows)
        for part, k in totals:
            at = pl.ds((part * carried + first + k) * rows, rows)
            totals[part, k] = totals[part, k] + ref[at] * factor
    for to, total in totals.items():
        out_ref[to] = total.astype(out_ref.dtype)


def add_up(own, received, first, cost):
    return pl.pallas_call(
        functools.partial(add_kernel, first),
        in_specs=[VMEM] * (1 + len(received)),
        out_specs=VMEM,
        out_shape=jax.ShapeDtypeStruct(own.shape, jnp.bfloat16),
        compiler_params=pltpu.CompilerParams(vmem_limit_bytes=SMALL),
        cost_estimate=pl.CostEstimate(flops=cost, bytes_accessed=0, transcendentals=0),
    )(own, *received)


def origin(n, step):
    me = lax.axis_index("pb")
    return me ^ step if n == 4 else (me - step) % n


def after(x, *others):
    return lax.optimization_barrier((x, *others))[0] if others else x


def phonon_part(steps, n_pb, table_ref, refs, first, k, rows=slice(None)):
    total = None
    p_own = table_ref.shape[2] // n_pb
    for step, head_ref, rest_ref in zip(steps, refs[::2], refs[1::2]):
        if p_own % 128:
            at = pl.ds(step * p_own, p_own)
        else:
            at = pl.ds(pl.multiple_of(origin(n_pb, step) * p_own, p_own), p_own)
        real, imag = [jnp.concatenate([head_ref[c, first + k], rest_ref[c, k]], 0) for c in range(2)]
        part = jnp.dot(table_ref[0, rows, at], jnp.concatenate([real, imag], 1), preferred_element_type=jnp.float32)
        part += jnp.dot(table_ref[1, rows, at], jnp.concatenate([-imag, real], 1), preferred_element_type=jnp.float32)
        total = part if total is None else total + part
    return total


def main_kernel(steps, n_pb, first, table_ref, *refs):
    out_ref = refs[-1]
    for k in range(out_ref.shape[0]):
        out_ref[k] = phonon_part(steps, n_pb, table_ref, refs[:-1], first, k)


def final_kernel(steps, n_pb, first, has_prior, table_ref, acc_ref, *refs):
    out_ref, staged, sems = refs[-3:]
    size, _, q, b = staged.shape
    copies = []
    for k in range(size):
        for h in range(PARTS):
            rows = pl.ds(h * (q // PARTS), q // PARTS)
            total = acc_ref[k, rows] + phonon_part(steps, n_pb, table_ref, refs[: -3 - has_prior], first, k, rows)
            staged[k, 0, rows] = total[:, :b]
            staged[k, 1, rows] = total[:, b:]
            copies.append(pltpu.make_async_copy(staged.at[k, :, rows], out_ref.at[first + k, :, rows], sems.at[k, h]))
            copies[-1].start()
    for copy in copies:
        copy.wait()


def kernel_inputs(blocks):
    return [step for step, _, _ in blocks], [x for _, head, rest in blocks for x in (head, rest)]


def phonon_main(n_pb, table, blocks, first):
    steps, flat = kernel_inputs(blocks)
    q = table.shape[1]
    _, size, rows, b = blocks[0][2].shape
    return pl.pallas_call(
        functools.partial(main_kernel, steps, n_pb, first),
        in_specs=[VMEM] * (1 + len(flat)),
        out_specs=VMEM,
        out_shape=jax.ShapeDtypeStruct((size, q, 2 * b), jnp.float32),
        compiler_params=pltpu.CompilerParams(vmem_limit_bytes=SMALL),
        cost_estimate=pl.CostEstimate(flops=PHON * q * rows * len(blocks) * b * size, bytes_accessed=0, transcendentals=0),
    )(table, *flat)


def phonon_final(n_pb, table, acc, blocks, prior, first, k_own):
    steps, flat = kernel_inputs(blocks)
    q = table.shape[1]
    _, size, rows, b = blocks[0][2].shape
    alias = [] if prior is None else [prior]
    return pl.pallas_call(
        functools.partial(final_kernel, steps, n_pb, first, len(alias)),
        in_specs=[VMEM] * (2 + len(flat)) + [HBM] * len(alias),
        out_specs=HBM,
        out_shape=jax.ShapeDtypeStruct((k_own, 2, q, b), jnp.float32),
        scratch_shapes=[pltpu.VMEM((size, 2, q, b), jnp.float32), pltpu.SemaphoreType.DMA((size, PARTS))],
        input_output_aliases={2 + len(flat): 0} if alias else {},
        compiler_params=pltpu.CompilerParams(vmem_limit_bytes=SMALL),
        cost_estimate=pl.CostEstimate(flops=PHON * q * rows * len(blocks) * b * size, bytes_accessed=size * q * b * 8, transcendentals=0),
    )(table, acc, *flat, *alias)


class Transfers:
    def __init__(self, n_re, n_pb, own, send):
        self.n_re, self.n_pb, self.own, self.send = n_re, n_pb, own, send
        self.made = {}
        self.steps = tuple(range(n_pb))

    def get(self, *what):
        if what not in self.made:
            self.made[what] = None
            self.made[what] = getattr(self, what[0])(*what[1:])
        return self.made[what]

    def gated(self, x, *what):
        gates = GATES.get(what, []) if self.n_pb == 4 else []
        return after(x, *[self.get(*other) for other in gates])

    def received(self, m):
        out = []
        for s in range(1, self.n_re):
            message = self.gated(self.send[s - 1][m].astype(jnp.float16), "received", m)
            out.append(lax.ppermute(message, "re", [(i, (i + s) % self.n_re) for i in range(self.n_re)]))
        return out

    def block(self, c):
        m, first = self.carrier[c]
        received = [self.gated(got, "block", c).astype(jnp.float32) for got in self.get("received", m)]
        return add_up(self.own[c], received, first, ADDCOST[c])

    def near(self, c):
        block = self.gated(self.get("block", c), "near", c)
        return lax.ppermute(block, "pb", [(i, i ^ 1) for i in range(self.n_pb)])

    def across(self, c):
        block = self.gated(self.get("block", c), "across", c)
        return lax.ppermute(block, "pb", [(i, i ^ 2) for i in range(self.n_pb)])

    def passed(self, c):
        return self.gated(self.get("across", c), "passed", c)

    def last(self, c):
        return lax.ppermute(self.get("passed", c), "pb", [(i, i ^ 1) for i in range(self.n_pb)])

    def shifted(self, c, s):
        return lax.ppermute(self.get("block", c), "pb", [(i, (i + s) % self.n_pb) for i in range(self.n_pb)])

    def step(self, c, s):
        if s == 0:
            return self.get("block", c)
        if self.n_pb == 4:
            return self.get({1: "near", 2: "across", 3: "last"}[s], c)
        return self.get("shifted", c, s)

    def blocks(self, c, steps):
        return [(s, self.step(0, s), self.step(c, s)) for s in steps]

    def acc(self, c):
        return phonon_main(self.n_pb, self.table, self.blocks(c, self.steps[:-1]), self.firsts[c])


def body(n_re, n_pb, g_wann, phonon_phase, electron_phase):
    k_own = electron_phase.shape[1] // n_re
    p_own = g_wann.shape[1]
    cuts = [k_own * c // sum(CUTS) for c in CUTS]
    ahead = p_own * HEAD[0] // HEAD[1] // (2 * GROUP) * (2 * GROUP)
    own, send = electron_sums(electron_phase, g_wann[:, :ahead], n_re, [k_own], [k_own], None, ahead)
    table = phonon_phase
    if p_own % 128 != 0:
        order = jnp.stack([origin(n_pb, step) for step in range(n_pb)])
        table = table.reshape(2, -1, n_pb, p_own)[:, :, order].reshape(table.shape)
    transfers = Transfers(n_re, n_pb, own, [list(a) for a in send])
    transfers.carrier = [(0, 0)]
    mcuts = [k_own * m // sum(MCUTS) for m in MCUTS]
    for c in range(len(cuts)):
        first = sum(cuts[:c])
        m = max(m for m in range(len(mcuts)) if sum(mcuts[:m]) <= first)
        transfers.carrier.append((1 + m, first - sum(mcuts[:m])))
    rest = electron_sums(after(electron_phase, own[0]), g_wann, n_re, cuts, mcuts, ahead, p_own - ahead)
    transfers.own = list(own) + list(rest[0])
    transfers.send = [list(a) + list(b) for a, b in zip(send, rest[1])]
    transfers.table = table
    transfers.firsts = [None] + [sum(cuts[:c]) for c in range(len(cuts))]
    result = None
    for c in range(1, 1 + len(cuts)):
        acc = transfers.get("acc", c)
        result = phonon_final(n_pb, table, acc, transfers.blocks(c, transfers.steps[-1:]), result, transfers.firsts[c], k_own)
    return result


def solution(mesh):
    return jax.shard_map(
        functools.partial(body, mesh.shape["re"], mesh.shape["pb"]),
        mesh=mesh,
        in_specs=(P(None, "pb", ("grp", "re"), "ka"), P(None, "pb", None), P()),
        out_specs=P(("grp", "re"), None, "pb", "ka"),
        check_vma=False,
    )
```

```python
import functools

import jax
import jax.numpy as jnp
from jax import lax
from jax.experimental import pallas as pl
from jax.experimental.pallas import tpu as pltpu
from jax.sharding import PartitionSpec as P

GROUP = 8
SIDE = 2
PIECES = 4
TAIL = 16
FULL = 32768.0
POWERS = (64, 32, 16, 8, 4, 2)
HEAD = (1, 4)
CUTS = (1, 1, 2)
ADDCOST = (0, 10**10, 10**10, 10**10)
GATES = {
    ("block", 1): [("block", 0)],
    ("block", 2): [("near", 0), ("across", 0)],
    ("block", 3): [("near", 0), ("across", 0)],
    ("passed", 0): [("near", 0)],
    ("passed", 1): [("passed", 0), ("block", 3), ("near", 1)],
    ("passed", 2): [("passed", 1), ("near", 2)],
    ("passed", 3): [("passed", 2)],
    ("received", 2): [("block", 0)],
}
MCUTS = (1, 3)
PHON = 80
PARTS = 4
SMALL = 16 * 2**20
LARGE = 50 * 2**20
VMEM = pl.BlockSpec(memory_space=pltpu.VMEM)
HBM = pl.BlockSpec(memory_space=pltpu.HBM)


def pick(me, n, choices):
    out = choices[0]
    for i in range(1, n):
        out = jnp.where(me == i, choices[i], out)
    return out


def phase_rows(me, n_re, phase_ref):
    k_all, e_all = phase_ref.shape[1:]
    e_own, k_own = e_all // n_re, k_all // n_re
    width = GROUP * e_own
    tables = []
    for part in range(2):
        full = phase_ref[part].astype(jnp.float32)
        own = pick(me, n_re, [full[:, r * e_own : (r + 1) * e_own] for r in range(n_re)])
        tables.append(jnp.concatenate([own] * GROUP, 1))
    row = lax.broadcasted_iota(jnp.int32, (k_own * GROUP, width), 0) % GROUP
    column = lax.broadcasted_iota(jnp.int32, (k_own * GROUP, width), 1) // e_own
    spread = []
    for table in tables:
        groups = [table[r * k_own : (r + 1) * k_own] for r in range(n_re)]
        moved = [pick(me, n_re, groups[s:] + groups[:s]) for s in range(n_re)]
        spread.append([
            jnp.where(row == column, jnp.broadcast_to(m[:, None], (k_own, GROUP, width)).reshape(k_own * GROUP, width), 0.0)
            for m in moved
        ])
    cos, sin = spread
    left = jnp.concatenate([x for s in range(n_re) for x in (cos[s], sin[s])], 0)
    right = jnp.concatenate([x for s in range(n_re) for x in (-sin[s], cos[s])], 0)
    return left.astype(jnp.bfloat16), right.astype(jnp.bfloat16)


def electron_kernel(n_re, cuts, mcuts, pieces, start, phase_ref, g_ref, *refs):
    n, m = len(cuts), len(mcuts)
    own_refs, send_refs = refs[:n], refs[n : n + (n_re - 1) * m]
    g_vmem, left_ref, right_ref, sems = ([g_ref] if pieces == 0 else []) + list(refs[n + (n_re - 1) * m :])
    _, rows, e_own, b = g_vmem.shape
    size = rows // max(pieces, 1)
    copies = [
        pltpu.make_async_copy(g_ref.at[:, pl.ds(start + i * size, size)], g_vmem.at[:, pl.ds(i * size, size)], sems.at[i])
        for i in range(pieces)
    ]
    for copy in copies:
        copy.start()
    left_ref[...], right_ref[...] = phase_rows(lax.axis_index("re"), n_re, phase_ref)
    depth = GROUP * e_own
    step = SIDE * GROUP
    largest = jnp.zeros((GROUP, b), jnp.float32)
    for i in range(rows // step):
        if pieces and i * step % size == 0:
            copies[i * step // size].wait()
        groups = [pl.ds(i * step + j * GROUP, GROUP) for j in range(SIDE)]
        real = jnp.concatenate([g_vmem[0, at].reshape(depth, b) for at in groups], 1)
        imag = jnp.concatenate([g_vmem[1, at].reshape(depth, b) for at in groups], 1)
        out = jnp.dot(left_ref[...], real, preferred_element_type=jnp.float32)
        out += jnp.dot(right_ref[...], imag, preferred_element_type=jnp.float32)
        out = out.reshape(n_re, 2, -1, GROUP, SIDE * b)
        if n_re > 1:
            sent = jnp.max(jnp.abs(out[1:].reshape(-1, GROUP, SIDE * b)), 0)
            for j in range(SIDE):
                largest = jnp.maximum(largest, sent[:, j * b : (j + 1) * b])
        for j, at in enumerate(groups):
            first = 0
            for c, kept in enumerate(cuts):
                own_refs[c][:, :, at] = out[0, :, first : first + kept, :, j * b : (j + 1) * b]
                first += kept
            first = 0
            for c, kept in enumerate(mcuts):
                for s in range(1, n_re):
                    for part in range(2):
                        for k in range(kept):
                            row = (part * kept + k) * rows + i * step + j * GROUP
                            send_refs[(s - 1) * m + c][pl.ds(row, GROUP)] = out[s, part, first + k, :, j * b : (j + 1) * b]
                first += kept
    if n_re > 1:
        top = jnp.max(largest, keepdims=True)
        scale, exponent = jnp.ones((1, 1), jnp.float32), jnp.zeros((1, 1), jnp.float32)
        for bit in POWERS:
            fits = top * scale * 2.0**bit <= FULL
            scale = jnp.where(fits, scale * 2.0**bit, scale)
            exponent = jnp.where(fits, exponent + bit, exponent)
        for ref in send_refs:
            last = ref.shape[0] - TAIL
            ref[pl.ds(0, last)] = ref[pl.ds(0, last)] * scale
            ref[pl.ds(last, TAIL)] = jnp.broadcast_to(exponent, (TAIL, b))


def electron_sums(phase, g_wann, n_re, cuts, mcuts, start, rows):
    _, _, e_own, b = g_wann.shape
    k_all = phase.shape[1]
    pieces = 0 if start is None else PIECES if rows % (PIECES * SIDE * GROUP) == 0 else 1
    own = [jax.ShapeDtypeStruct((2, size, rows, b), jnp.float32) for size in cuts]
    send = [jax.ShapeDtypeStruct((2 * size * rows + TAIL, b), jnp.float32) for _ in range(n_re - 1) for size in mcuts]
    outs = pl.pallas_call(
        functools.partial(electron_kernel, n_re, cuts, mcuts, pieces, start),
        in_specs=[VMEM, HBM if pieces else VMEM],
        out_specs=[VMEM] * len(own + send),
        out_shape=own + send,
        scratch_shapes=([pltpu.VMEM((2, rows, e_own, b), g_wann.dtype)] if pieces else [])
        + [
            pltpu.VMEM((2 * k_all * GROUP, GROUP * e_own), jnp.bfloat16),
            pltpu.VMEM((2 * k_all * GROUP, GROUP * e_own), jnp.bfloat16),
            pltpu.SemaphoreType.DMA((max(pieces, 1),)),
        ],
        compiler_params=pltpu.CompilerParams(vmem_limit_bytes=LARGE if pieces else SMALL),
        cost_estimate=pl.CostEstimate(flops=8 * k_all * e_own * rows * b, bytes_accessed=4 * rows * e_own * b, transcendentals=0),
    )(phase, g_wann)
    return outs[: len(cuts)], [outs[len(cuts) + s * len(mcuts) : len(cuts) + (s + 1) * len(mcuts)] for s in range(n_re - 1)]


def add_kernel(first, own_ref, *refs):
    out_ref = refs[-1]
    _, kept, rows, _ = own_ref.shape
    totals = {(part, k): own_ref[part, k] for part in range(2) for k in range(kept)}
    for ref in refs[:-1]:
        exponent = ref[pl.ds(ref.shape[0] - TAIL, 1)]
        factor = jnp.ones_like(exponent)
        for bit in POWERS:
            taken = exponent >= bit
            exponent = jnp.where(taken, exponent - bit, exponent)
            factor = jnp.where(taken, factor * 2.0**-bit, factor)
        carried = (ref.shape[0] - TAIL) // (2 * rows)
        for part, k in totals:
            at = pl.ds((part * carried + first + k) * rows, rows)
            totals[part, k] = totals[part, k] + ref[at] * factor
    for to, total in totals.items():
        out_ref[to] = total.astype(out_ref.dtype)


def add_up(own, received, first, cost):
    return pl.pallas_call(
        functools.partial(add_kernel, first),
        in_specs=[VMEM] * (1 + len(received)),
        out_specs=VMEM,
        out_shape=jax.ShapeDtypeStruct(own.shape, jnp.bfloat16),
        compiler_params=pltpu.CompilerParams(vmem_limit_bytes=SMALL),
        cost_estimate=pl.CostEstimate(flops=cost, bytes_accessed=0, transcendentals=0),
    )(own, *received)


def origin(n, step):
    me = lax.axis_index("pb")
    return me ^ step if n == 4 else (me - step) % n


def after(x, *others):
    return lax.optimization_barrier((x, *others))[0] if others else x


def phonon_part(steps, n_pb, table_ref, refs, first, k, rows=slice(None)):
    total = None
    p_own = table_ref.shape[2] // n_pb
    for step, head_ref, rest_ref in zip(steps, refs[::2], refs[1::2]):
        if p_own % 128:
            at = pl.ds(step * p_own, p_own)
        else:
            at = pl.ds(pl.multiple_of(origin(n_pb, step) * p_own, p_own), p_own)
        real, imag = [jnp.concatenate([head_ref[c, first + k], rest_ref[c, k]], 0) for c in range(2)]
        part = jnp.dot(table_ref[0, rows, at], jnp.concatenate([real, imag], 1), preferred_element_type=jnp.float32)
        part += jnp.dot(table_ref[1, rows, at], jnp.concatenate([-imag, real], 1), preferred_element_type=jnp.float32)
        total = part if total is None else total + part
    return total


def main_kernel(steps, n_pb, first, table_ref, *refs):
    out_ref = refs[-1]
    for k in range(out_ref.shape[0]):
        out_ref[k] = phonon_part(steps, n_pb, table_ref, refs[:-1], first, k)


def final_kernel(steps, n_pb, first, has_prior, table_ref, acc_ref, *refs):
    out_ref, staged, sems = refs[-3:]
    size, _, q, b = staged.shape
    copies = []
    for k in range(size):
        for h in range(PARTS):
            rows = pl.ds(h * (q // PARTS), q // PARTS)
            total = acc_ref[k, rows] + phonon_part(steps, n_pb, table_ref, refs[: -3 - has_prior], first, k, rows)
            staged[k, 0, rows] = total[:, :b]
            staged[k, 1, rows] = total[:, b:]
            copies.append(pltpu.make_async_copy(staged.at[k, :, rows], out_ref.at[first + k, :, rows], sems.at[k, h]))
            copies[-1].start()
    for copy in copies:
        copy.wait()


def kernel_inputs(blocks):
    return [step for step, _, _ in blocks], [x for _, head, rest in blocks for x in (head, rest)]


def phonon_main(n_pb, table, blocks, first):
    steps, flat = kernel_inputs(blocks)
    q = table.shape[1]
    _, size, rows, b = blocks[0][2].shape
    return pl.pallas_call(
        functools.partial(main_kernel, steps, n_pb, first),
        in_specs=[VMEM] * (1 + len(flat)),
        out_specs=VMEM,
        out_shape=jax.ShapeDtypeStruct((size, q, 2 * b), jnp.float32),
        compiler_params=pltpu.CompilerParams(vmem_limit_bytes=SMALL),
        cost_estimate=pl.CostEstimate(flops=PHON * q * rows * len(blocks) * b * size, bytes_accessed=0, transcendentals=0),
    )(table, *flat)


def phonon_final(n_pb, table, acc, blocks, prior, first, k_own):
    steps, flat = kernel_inputs(blocks)
    q = table.shape[1]
    _, size, rows, b = blocks[0][2].shape
    alias = [] if prior is None else [prior]
    return pl.pallas_call(
        functools.partial(final_kernel, steps, n_pb, first, len(alias)),
        in_specs=[VMEM] * (2 + len(flat)) + [HBM] * len(alias),
        out_specs=HBM,
        out_shape=jax.ShapeDtypeStruct((k_own, 2, q, b), jnp.float32),
        scratch_shapes=[pltpu.VMEM((size, 2, q, b), jnp.float32), pltpu.SemaphoreType.DMA((size, PARTS))],
        input_output_aliases={2 + len(flat): 0} if alias else {},
        compiler_params=pltpu.CompilerParams(vmem_limit_bytes=SMALL),
        cost_estimate=pl.CostEstimate(flops=PHON * q * rows * len(blocks) * b * size, bytes_accessed=size * q * b * 8, transcendentals=0),
    )(table, acc, *flat, *alias)


class Transfers:
    def __init__(self, n_re, n_pb, own, send):
        self.n_re, self.n_pb, self.own, self.send = n_re, n_pb, own, send
        self.made = {}
        self.steps = tuple(range(n_pb))

    def get(self, *what):
        if what not in self.made:
            self.made[what] = None
            self.made[what] = getattr(self, what[0])(*what[1:])
        return self.made[what]

    def gated(self, x, *what):
        gates = GATES.get(what, []) if self.n_pb == 4 else []
        return after(x, *[self.get(*other) for other in gates])

    def received(self, m):
        out = []
        for s in range(1, self.n_re):
            message = self.gated(self.send[s - 1][m].astype(jnp.float16), "received", m)
            out.append(lax.ppermute(message, "re", [(i, (i + s) % self.n_re) for i in range(self.n_re)]))
        return out

    def block(self, c):
        m, first = self.carrier[c]
        received = [self.gated(got, "block", c).astype(jnp.float32) for got in self.get("received", m)]
        return add_up(self.own[c], received, first, ADDCOST[c])

    def near(self, c):
        block = self.gated(self.get("block", c), "near", c)
        return lax.ppermute(block, "pb", [(i, i ^ 1) for i in range(self.n_pb)])

    def across(self, c):
        block = self.gated(self.get("block", c), "across", c)
        return lax.ppermute(block, "pb", [(i, i ^ 2) for i in range(self.n_pb)])

    def passed(self, c):
        return self.gated(self.get("across", c), "passed", c)

    def last(self, c):
        return lax.ppermute(self.get("passed", c), "pb", [(i, i ^ 1) for i in range(self.n_pb)])

    def shifted(self, c, s):
        return lax.ppermute(self.get("block", c), "pb", [(i, (i + s) % self.n_pb) for i in range(self.n_pb)])

    def step(self, c, s):
        if s == 0:
            return self.get("block", c)
        if self.n_pb == 4:
            return self.get({1: "near", 2: "across", 3: "last"}[s], c)
        return self.get("shifted", c, s)

    def blocks(self, c, steps):
        return [(s, self.step(0, s), self.step(c, s)) for s in steps]

    def acc(self, c):
        return phonon_main(self.n_pb, self.table, self.blocks(c, self.steps[:-1]), self.firsts[c])


def body(n_re, n_pb, g_wann, phonon_phase, electron_phase):
    k_own = electron_phase.shape[1] // n_re
    p_own = g_wann.shape[1]
    cuts = [k_own * c // sum(CUTS) for c in CUTS]
    ahead = p_own * HEAD[0] // HEAD[1] // (2 * GROUP) * (2 * GROUP)
    own, send = electron_sums(electron_phase, g_wann[:, :ahead], n_re, [k_own], [k_own], None, ahead)
    table = phonon_phase
    if p_own % 128 != 0:
        order = jnp.stack([origin(n_pb, step) for step in range(n_pb)])
        table = table.reshape(2, -1, n_pb, p_own)[:, :, order].reshape(table.shape)
    transfers = Transfers(n_re, n_pb, own, [list(a) for a in send])
    transfers.carrier = [(0, 0)]
    mcuts = [k_own * m // sum(MCUTS) for m in MCUTS]
    for c in range(len(cuts)):
        first = sum(cuts[:c])
        m = max(m for m in range(len(mcuts)) if sum(mcuts[:m]) <= first)
        transfers.carrier.append((1 + m, first - sum(mcuts[:m])))
    rest = electron_sums(after(electron_phase, own[0]), g_wann, n_re, cuts, mcuts, ahead, p_own - ahead)
    transfers.own = list(own) + list(rest[0])
    transfers.send = [list(a) + list(b) for a, b in zip(send, rest[1])]
    transfers.table = table
    transfers.firsts = [None] + [sum(cuts[:c]) for c in range(len(cuts))]
    result = None
    for c in range(1, 1 + len(cuts)):
        acc = transfers.get("acc", c)
        result = phonon_final(n_pb, table, acc, transfers.blocks(c, transfers.steps[-1:]), result, transfers.firsts[c], k_own)
    return result


def solution(mesh):
    return jax.shard_map(
        functools.partial(body, mesh.shape["re"], mesh.shape["pb"]),
        mesh=mesh,
        in_specs=(P(None, "pb", ("grp", "re"), "ka"), P(None, "pb", None), P()),
        out_specs=P(("grp", "re"), None, "pb", "ka"),
        check_vma=False,
    )
```
